256 devices in a mesh: dp: 4 (over z_hi, core), mp: 64 (over z_lo, x, y).
Axes of the slice: x: 4, y: 4, z: 8 (z_hi: 2, z_lo: 4; z = z_hi * 4 + z_lo), core: 2. Of those that a mesh axis runs over, the one named last changes fastest.
Arguments:
- inputs: bfloat16 [512, 6144], P(('dp', 'mp')), may hold values from -6 to 6
- out_grad: bfloat16 [512, 6144], P(('dp', 'mp')), may hold values from -1.1953125 to 1.1953125
- pre_act: bfloat16 [512, 32768], P('dp', 'mp'), may hold values from -8 to 8
- norm_gain: float32 [6144], replicated, may hold values from 0.25 to 1.75
- up_weight: bfloat16 [128, 4096, 256], P('mp'), may hold values from -0.09375 to 0.09375
- down_weight: bfloat16 [128, 256, 4096], P('mp'), may hold values from -0.09375 to 0.09375
- row_blocks: int32 [128, 16], replicated, may hold values from 0 to 23, as said below
- col_blocks: int32 [128, 16], replicated, may hold values from 0 to 23, as said below
- counts: int32 [64], replicated, may hold values from 0 to 2, as said below
Outputs:
- grad_input: bfloat16 [512, 6144], P(('dp', 'mp'))
- up_grad: bfloat16 [128, 4096, 256], P('mp', 'dp')
- down_grad: bfloat16 [128, 256, 4096], P('mp', 'dp')
The draws below stay inside these ranges and needn't reach their ends.
Inputs may be any that keep to these rules, and one draw needn't show every extreme that they name: `row_blocks`: each row holds distinct feature blocks in increasing order. `col_blocks`: each row holds distinct feature blocks in increasing order. counts[i] + counts[i + 32] <= 2 for i < 32, and some device has 2.
All inputs are finite; a program needn't handle non-finite values.
Results may differ from the reference program's by a relative error of at most 0.013.
Values may be sent and summed in bfloat16 or wider, within the bound.
A program may use at most 128 MiB of HBM per device.

```python
import jax
import jax.numpy as jnp
from jax import lax

D = 6144
BLK = 256
SLOTS = 2
KR = 16
KC = 16
DB = 24
TOKENS = 512
N_DP = 4
N_MP = 64


def kept_blocks(key, kept):
    scores = jax.random.randint(key, (N_MP * SLOTS, DB), 0, 1 << 20) * DB + jnp.arange(DB, dtype=jnp.int32)[None, :]
    order = jnp.argsort(scores, axis=1, stable=True)[:, :kept]
    return jnp.sort(order, axis=1).astype(jnp.int32)


def draw_row_blocks(key, part):
    key = jax.random.fold_in(key, 11)
    return kept_blocks(key, KR)


def draw_col_blocks(key, part):
    key = jax.random.fold_in(key, 23)
    return kept_blocks(key, KC)


def draw_counts(key, part):
    key = jax.random.fold_in(key, 37)
    first_key, second_key = jax.random.split(key)
    pattern = jax.random.randint(first_key, (N_MP // 2,), 0, 5)
    pattern = pattern.at[0].set(jax.random.randint(second_key, (), 0, 2))
    lower_table = jnp.array([2, 0, 1, 1, 0], jnp.int32)
    upper_table = jnp.array([0, 2, 1, 0, 1], jnp.int32)
    return jnp.concatenate([jnp.take(lower_table, pattern), jnp.take(upper_table, pattern)]).astype(jnp.int32)


def block_levels(stream_key, dims, cuts, low, top_value):
    factor_of = 1.0
    for dim, shards_of in cuts:
        steps = jax.random.uniform(jax.random.fold_in(jax.random.fold_in(stream_key, 6), dim), (shards_of,), jnp.float32, low / len(cuts), top_value / len(cuts))
        factor_of = factor_of * jnp.repeat(jnp.exp(steps), dims[dim] // shards_of).reshape((-1,) + (1,) * (len(dims) - 1 - dim))
    return factor_of


def normal_values(stream_key, extent, deviation, limit, pieces=(), kind=jnp.bfloat16):
    drawn = deviation * jax.random.normal(stream_key, extent, jnp.float32)
    if pieces:
        drawn = drawn * block_levels(stream_key, extent, pieces, -0.22, 0.18)
    return jnp.clip(drawn, -limit, limit).astype(kind)


def setup_inputs(seed: int = 0) -> dict:
    keys = jax.random.split(jax.random.key(seed), 10)
    inputs = normal_values(keys[0], (TOKENS, D), 1.0, 6.0, ((0, 256),))
    out_grad = normal_values(keys[1], (TOKENS, D), 0.2, 1.1953125, ((0, 256),))
    pre_act = normal_values(keys[2], (TOKENS, N_MP * SLOTS * BLK), 1.5, 8.0, ((0, 4), (1, 64)))
    norm_gain = jnp.clip(1.0 + 0.15 * jax.random.normal(keys[3], (D,), jnp.float32), 0.25, 1.75)
    up_weight = normal_values(keys[4], (N_MP * SLOTS, KR * BLK, BLK), (KR * BLK) ** -0.5, 0.09375, ((0, 64),))
    down_weight = normal_values(keys[5], (N_MP * SLOTS, BLK, KC * BLK), (KC * BLK) ** -0.5, 0.09375, ((0, 64),))
    row_blocks = draw_row_blocks(jax.random.fold_in(keys[9], 71), 0)
    col_blocks = draw_col_blocks(jax.random.fold_in(keys[9], 71), 0)
    counts = draw_counts(jax.random.fold_in(keys[9], 71), 0)
    return {"inputs": inputs, "out_grad": out_grad, "pre_act": pre_act, "norm_gain": norm_gain, "up_weight": up_weight, "down_weight": down_weight, "row_blocks": row_blocks, "col_blocks": col_blocks, "counts": counts}


EPS = 1e-06

def normalize(inputs, norm_gain):
    widened = inputs.astype(jnp.float32)
    average = lax.optimization_barrier(jnp.mean(widened, axis=-1, keepdims=True))
    centred = widened - average
    inv_std = lax.rsqrt(lax.optimization_barrier(jnp.mean(centred * centred, axis=-1, keepdims=True)) + EPS)
    unit_rows = centred * inv_std
    return (unit_rows, inv_std, (unit_rows * norm_gain).astype(jnp.bfloat16))

def reference(inputs, out_grad, pre_act, norm_gain, up_weight, down_weight, row_blocks, col_blocks, counts):
    unit_rows, inv_std, normed = normalize(inputs, norm_gain)
    block_count = D // BLK
    group_rows = TOKENS // N_DP
    normed_blocks = normed.reshape(TOKENS, block_count, BLK)
    grad_blocks = out_grad.reshape(TOKENS, block_count, BLK)

    def one_slot(accum_grad, slot_index):
        active = slot_index % SLOTS < counts[slot_index // SLOTS]

        def work(accum_grad):
            pre_block = lax.dynamic_slice_in_dim(pre_act, slot_index * BLK, BLK, 1)
            row_ids = row_blocks[slot_index]
            col_ids = col_blocks[slot_index]
            picked = jnp.take(normed_blocks, row_ids, axis=1).reshape(TOKENS, KR * BLK)
            seen = jnp.take(grad_blocks, col_ids, axis=1).reshape(TOKENS, KC * BLK)
            act_grad = jnp.dot(seen, down_weight[slot_index].T, preferred_element_type=jnp.float32)
            activated, pullback = jax.vjp(jax.nn.gelu, pre_block.astype(jnp.float32))
            pre_grad = pullback(act_grad)[0].astype(jnp.bfloat16)
            activated = activated.astype(jnp.bfloat16)
            up_sum = jnp.zeros((KR * BLK, BLK), jnp.float32)
            down_sum = jnp.zeros((BLK, KC * BLK), jnp.float32)
            for group_index in range(N_DP):
                lower = group_index * group_rows
                upper = lower + group_rows
                up_part = jnp.dot(picked[lower:upper].T, pre_grad[lower:upper], preferred_element_type=jnp.float32)
                down_part = jnp.dot(activated[lower:upper].T, seen[lower:upper], preferred_element_type=jnp.float32)
                up_sum = up_sum + lax.optimization_barrier(up_part.astype(jnp.bfloat16)).astype(jnp.float32)
                down_sum = down_sum + lax.optimization_barrier(down_part.astype(jnp.bfloat16)).astype(jnp.float32)
            row_term = jnp.dot(pre_grad, up_weight[slot_index].T, preferred_element_type=jnp.float32)
            accum_grad = accum_grad.at[:, row_ids].add(row_term.reshape(TOKENS, KR, BLK))
            return (accum_grad, (up_sum.astype(jnp.bfloat16), down_sum.astype(jnp.bfloat16)))

        def skip(accum_grad):
            return (accum_grad, (jnp.zeros((KR * BLK, BLK), jnp.bfloat16), jnp.zeros((BLK, KC * BLK), jnp.bfloat16)))
        return lax.cond(active, work, skip, accum_grad)
    start_grad = jnp.zeros((TOKENS, block_count, BLK), jnp.float32)
    normed_grad, (up_grad, down_grad) = lax.scan(one_slot, start_grad, jnp.arange(N_MP * SLOTS, dtype=jnp.int32))
    scaled = normed_grad.reshape(TOKENS, D) * norm_gain
    grad_input = inv_std * (scaled - lax.optimization_barrier(jnp.mean(scaled, axis=-1, keepdims=True)) - unit_rows * lax.optimization_barrier(jnp.mean(scaled * unit_rows, axis=-1, keepdims=True)))
    return (grad_input.astype(jnp.bfloat16), up_grad, down_grad)
```

```python
import math

import jax
import jax.numpy as jnp
from jax import lax
from jax.experimental import pallas as pl
from jax.experimental.pallas import tpu as pltpu
from jax.sharding import PartitionSpec as P

EPS = 1e-06
F32 = jnp.float32
BF16 = jnp.bfloat16
PIECES = 8
PIECE = 768
BLK = 256
SLOTS = 2
KEPT = 16
FEATURES = 6144
N_COPIES = 80


def dot(a, b, dims):
    return lax.dot_general(a, b, (dims, ((), ())), preferred_element_type=F32)


def select_rows(rows, columns, source_of):
    r = lax.broadcasted_iota(jnp.int32, (rows, columns), 0)
    c = lax.broadcasted_iota(jnp.int32, (rows, columns), 1)
    return (c == source_of(r)).astype(BF16)


def gelu_pair(z):
    a = math.sqrt(2.0 / math.pi)
    z2 = z * z
    t = jnp.tanh(a * z * (1.0 + 0.044715 * z2))
    half = 0.5 * (1.0 + t)
    slope = half + 0.5 * z * (1.0 - t * t) * (a * (1.0 + 3.0 * 0.044715 * z2))
    return z * half, slope


def kernel(
    x_ref, og_ref, pre_hbm, gain_ref, up_hbm, dn_hbm, row_ref, col_ref, cnt_ref,
    gin_ref, upg_ref, dng_ref,
    up, dn, pre, pa,
    pack, gain16, unit16, inv16,
    zraw_og, zraw_nm,
    og_own, og_sib, nm_own, nm_sib,
    acc, act, pg, pgh, pgb,
    ra, rb, fa1, fa2, fb1, fb2, ga1, ga2, gb1, gb2,
    ya, xb, ha1, ha2, hb1, hb2, ka1, ka2, kb1, kb2,
    zs, zr, pos,
    local_sem, send_sem, recv_sem,
):
    dp = lax.axis_index("dp")
    mp = lax.axis_index("mp")
    h, c = lax.div(dp, 2), lax.rem(dp, 2)
    z, x, y = lax.div(mp, 16), lax.rem(lax.div(mp, 4), 4), lax.rem(mp, 4)
    z8 = h * 4 + z
    xp, xm, xo = lax.rem(x + 1, 4), lax.rem(x + 3, 4), lax.rem(x + 2, 4)
    yp, ym, yo = lax.rem(y + 1, 4), lax.rem(y + 3, 4), lax.rem(y + 2, 4)

    def device(h=h, c=c, z=z, x=x, y=y):
        return {"dp": h * 2 + c, "mp": z * 16 + x * 4 + y}

    def z_device(at):
        return device(h=lax.div(at, 4), z=lax.rem(at, 4))

    x_plus, x_minus = device(x=xp), device(x=xm)
    y_plus, y_minus = device(y=yp), device(y=ym)
    sibling = device(c=1 - c)
    partner = device(h=1 - h)

    started = []
    count = [0]

    def send(src, dst, target):
        k = count[0]
        count[0] += 1
        copy = pltpu.make_async_remote_copy(
            src_ref=src, dst_ref=dst, send_sem=send_sem.at[k], recv_sem=recv_sem.at[k],
            device_id=target, device_id_type=pl.DeviceIdType.MESH,
        )
        copy.start()
        started.append(copy)
        return k

    def arrive(k, dst):
        pltpu.make_async_remote_copy(
            src_ref=dst, dst_ref=dst, send_sem=send_sem.at[k], recv_sem=recv_sem.at[k],
            device_id=sibling, device_id_type=pl.DeviceIdType.MESH,
        ).wait_recv()

    up_copies = [
        pltpu.make_async_copy(up_hbm.at[s], up.at[s, pl.ds(0, KEPT)], local_sem.at[s])
        for s in range(SLOTS)
    ]
    dn_copy = pltpu.make_async_copy(dn_hbm, dn, local_sem.at[2])
    pre_copy = pltpu.make_async_copy(pre_hbm, pre, local_sem.at[3])
    pre_copy.start()
    dn_copy.start()
    for copy in up_copies:
        copy.start()

    barrier = pltpu.get_barrier_semaphore()
    greeted = [z_device(lax.rem(z8 + k, 8)) for k in range(1, 8)]
    greeted += [x_plus, x_minus, y_plus, y_minus, sibling]
    for target in greeted:
        pl.semaphore_signal(
            barrier, inc=1, device_id=target, device_id_type=pl.DeviceIdType.MESH
        )

    for p in range(PIECES):
        pack[2 * p : 2 * p + 2, :] = og_ref[:, p * PIECE : (p + 1) * PIECE].astype(F32)
    zraw_og[z8] = pack[...].astype(BF16)
    for p in range(PIECES):
        pack[2 * p : 2 * p + 2, :] = x_ref[:, p * PIECE : (p + 1) * PIECE].astype(F32)
        gain16[2 * p : 2 * p + 2, :] = jnp.broadcast_to(
            gain_ref[:, p * PIECE : (p + 1) * PIECE], (2, PIECE)
        )
    first = lax.rem(lax.broadcasted_iota(jnp.int32, (16, 1), 0), 2) == 0

    def token_mean(values):
        rows = jnp.sum(values, axis=1, keepdims=True)
        total0 = jnp.sum(jnp.where(first, rows, 0.0), axis=0, keepdims=True)
        total1 = jnp.sum(jnp.where(first, 0.0, rows), axis=0, keepdims=True)
        return jnp.where(first, total0, total1) * (1.0 / FEATURES)

    widened = pack[...]
    centred = widened - token_mean(widened)
    inv_std = lax.rsqrt(token_mean(centred * centred) + EPS)
    unit_rows = centred * inv_std
    unit16[...] = unit_rows
    inv16[...] = jnp.broadcast_to(inv_std, (16, 128))
    zraw_nm[z8] = (unit_rows * gain16[...]).astype(BF16)

    pl.semaphore_wait(barrier, len(greeted))

    def z_send(raw):
        return [
            (k, send(raw.at[z8], raw.at[z8], z_device(lax.rem(z8 + k, 8)))) for k in range(1, 8)
        ]

    og_z = z_send(zraw_og)
    nm_z = z_send(zraw_nm)

    pre_copy.wait()
    order = select_rows(
        128, 128, lambda r: lax.div(lax.rem(r, 8), 2) * 32 + lax.div(r, 8) * 2 + lax.rem(r, 2)
    )
    pa[0, h] = dot(order, pre[...], ((1,), (0,))).astype(BF16)
    pa_sib = send(pa.at[0, h], pa.at[1, h], sibling)
    pa_part = send(pa.at[0, h], pa.at[0, h], partner)

    def place(raw, gathered, arrivals):
        for k, sem in arrivals:
            arrive(sem, raw.at[lax.rem(z8 + 8 - k, 8)])
        order = select_rows(
            128, 128, lambda r: lax.div(lax.rem(r, 16), 2) * 16 + lax.div(r, 16) * 2 + lax.rem(r, 2)
        )
        tiles = dot(order, raw[...].reshape(128, PIECE), ((1,), (0,))).astype(BF16)
        for p in range(PIECES):
            for q in range(PIECE // 128):
                gathered[p * 6 + q, x, y] = tiles[16 * p : 16 * p + 16, 128 * q : 128 * q + 128]

    lo, lo1, lo2 = pl.ds(0, 24), pl.ds(0, 12), pl.ds(12, 12)
    hi, hi1, hi2 = pl.ds(24, 24), pl.ds(24, 12), pl.ds(36, 12)

    def ring_a(g, lane, at):
        return g.at[lane, at, y]

    def ring_b(g, lane, at):
        return g.at[lane, x, at]

    def wide_a(g, lane, at):
        return g.at[lane, :, at]

    def wide_b(g, lane, at):
        return g.at[lane, at]

    def spread(view, g, lane, at, plus, minus):
        mine = view(g, lane, at)
        return send(mine, mine, plus), send(mine, mine, minus)

    def relay(view, g, lanes, sems, at_p, at_m, plus, minus):
        lane, lane1, lane2 = lanes
        arrive(sems[0], view(g, lane, at_m))
        one = send(view(g, lane1, at_m), view(g, lane1, at_m), plus)
        arrive(sems[1], view(g, lane, at_p))
        two = send(view(g, lane2, at_p), view(g, lane2, at_p), minus)
        return one, two

    def finish(view, g, lanes, sems, at_o):
        arrive(sems[0], view(g, lanes[1], at_o))
        arrive(sems[1], view(g, lanes[2], at_o))

    lanes_a, lanes_b = (lo, lo1, lo2), (hi, hi1, hi2)

    def narrow_spread(g):
        return (
            spread(ring_a, g, lo, x, x_plus, x_minus),
            spread(ring_b, g, hi, y, y_plus, y_minus),
        )

    def narrow_relay(g, sems):
        return (
            relay(ring_a, g, lanes_a, sems[0], xp, xm, x_plus, x_minus),
            relay(ring_b, g, lanes_b, sems[1], yp, ym, y_plus, y_minus),
        )

    def narrow_finish(g, sems):
        finish(ring_a, g, lanes_a, sems[0], xo)
        finish(ring_b, g, lanes_b, sems[1], yo)

    def wide_spread(g):
        return (
            spread(wide_a, g, lo, y, y_plus, y_minus),
            spread(wide_b, g, hi, x, x_plus, x_minus),
        )

    def wide_relay(g, sems):
        return (
            relay(wide_a, g, lanes_a, sems[0], yp, ym, y_plus, y_minus),
            relay(wide_b, g, lanes_b, sems[1], xp, xm, x_plus, x_minus),
        )

    def wide_finish(g, sems):
        finish(wide_a, g, lanes_a, sems[0], yo)
        finish(wide_b, g, lanes_b, sems[1], xo)

    place(zraw_og, og_own, og_z)
    og_n1 = narrow_spread(og_own)
    place(zraw_nm, nm_own, nm_z)
    nm_n1 = narrow_spread(nm_own)
    og_n2 = narrow_relay(og_own, og_n1)
    nm_n2 = narrow_relay(nm_own, nm_n1)

    for s in range(SLOTS):
        up[s, KEPT] = jnp.zeros((BLK, BLK), BF16)

    def locate(b, carry):
        for s in range(SLOTS):
            found = jnp.int32(KEPT)
            for k in range(KEPT):
                found = jnp.where(row_ref[2 * mp + s, k] == b, k, found)
            pos[s * 24 + b] = found
        return carry

    narrow_finish(og_own, og_n2)
    og_w1 = wide_spread(og_own)
    lax.fori_loop(0, 24, locate, 0)
    arrive(pa_part, pa.at[0, 1 - h])
    pa_fwd = send(pa.at[0, 1 - h], pa.at[1, 1 - h], sibling)
    narrow_finish(nm_own, nm_n2)
    og_w2 = wide_relay(og_own, og_w1)
    nm_w1 = wide_spread(nm_own)
    dn_copy.wait()
    for copy in up_copies:
        copy.wait()
    wide_finish(og_own, og_w2)
    og_s = send(og_own, og_sib, sibling)

    live = [s < cnt_ref[mp] for s in range(SLOTS)]

    def tokens(g, b):
        return jnp.concatenate([g[2 * b], g[2 * b + 1]], axis=-1).reshape(BLK, BLK)

    def back(g, group):
        for s in range(SLOTS):

            def grow(k, carry):
                parts = [tokens(g, col_ref[2 * mp + s, 4 * k + j]) for j in range(4)]
                start = pl.multiple_of(k * 1024, 1024)
                term = dot(
                    jnp.concatenate(parts, axis=1), dn[s, :, pl.ds(start, 1024)], ((1,), (1,))
                )

                @pl.when(k == 0)
                def _():
                    acc[s] = term

                @pl.when(k > 0)
                def _():
                    acc[s] += term

                return carry

            lax.fori_loop(0, KEPT // 4, grow, 0)
        mine = h == 0

        def derive(j, carry):
            at32 = pl.multiple_of(j * 32, 32)
            at16 = pl.multiple_of(j * 16, 16)
            rows32 = pl.multiple_of(group * 256 + j * 32, 32)
            for s in range(SLOTS):
                lanes = slice(s * BLK, (s + 1) * BLK)
                grads = acc[s, pl.ds(at32, 32), :].reshape(2, 2, 8, BLK)
                kept, acts = [], []
                for half in range(2):
                    value, slope = gelu_pair(pa[group, half, pl.ds(at16, 16), lanes].astype(F32))
                    grad = grads[:, half].reshape(16, BLK) * slope
                    kept.append(jnp.where(live[s], grad, 0.0))
                    acts.append(jnp.where(live[s], value, 0.0).reshape(2, 8, BLK))
                if group == 0:
                    pgh[pl.ds(at16, 16), lanes] = jnp.where(mine, kept[0], kept[1]).astype(BF16)
                kept = [part.reshape(2, 8, BLK) for part in kept]
                pg[pl.ds(rows32, 32), lanes] = jnp.stack(kept, 1).reshape(32, BLK).astype(BF16)
                act[pl.ds(rows32, 32), lanes] = jnp.stack(acts, 1).reshape(32, BLK).astype(BF16)
            return carry

        lax.fori_loop(0, 8, derive, 0)

    back(og_own, 0)

    order = select_rows(
        128, 128, lambda r: lax.div(lax.rem(r, 32), 8) * 32 + lax.div(r, 32) * 8 + lax.rem(r, 8)
    )
    pgb[...] = dot(order, pgh[...], ((1,), (0,))).astype(BF16)

    def terms(source, out, base):
        def one(b, carry):
            weights = [up[s, pos[s * 24 + base + b]] for s in range(SLOTS)]
            term = dot(source[...], jnp.concatenate(weights, axis=1), ((1,), (1,))).astype(BF16)
            for q in range(4):
                out[q, b] = term[32 * q : 32 * q + 32]
            return carry

        lax.fori_loop(0, 12, one, 0)

    def reduce_start(r, half, at_o, f1, f2, plus, minus):
        n = half * 2
        return (
            send(r.at[at_o, pl.ds(0, half)], f1, plus),
            send(r.at[at_o, pl.ds(half, n - half)], f2, minus),
        )

    def reduce_relay(r, half, sems, at_p, at_m, f1, f2, g1, g2, plus, minus):
        arrive(sems[0], f1)
        for j in range(half):
            r[at_p, j] = (r[at_p, j].astype(F32) + f1[j].astype(F32)).astype(BF16)
        one = send(r.at[at_p], g1, plus)
        arrive(sems[1], f2)
        for j in range(half):
            r[at_m, half + j] = (r[at_m, half + j].astype(F32) + f2[j].astype(F32)).astype(BF16)
        two = send(r.at[at_m], g2, minus)
        return one, two

    def repack(r, sems, at, g1, g2, out):
        arrive(sems[0], g1)
        arrive(sems[1], g2)
        for j in range(6):
            top, low = [
                r[at, b].astype(F32) + g1[b].astype(F32) + g2[b].astype(F32) for b in (j, 6 + j)
            ]
            for q in range(4):
                rows = slice(8 * q, 8 * q + 8)
                out[q, j] = jnp.concatenate([top[rows], low[rows]], axis=0).astype(BF16)

    terms(pgh, ra, 0)
    a1 = reduce_start(ra, 6, xo, fa1, fa2, x_plus, x_minus)
    terms(pgb, rb, 12)
    b1 = reduce_start(rb, 6, yo, fb1, fb2, y_plus, y_minus)
    nm_w2 = wide_relay(nm_own, nm_w1)
    a2 = reduce_relay(ra, 6, a1, xp, xm, fa1, fa2, ga1, ga2, x_plus, x_minus)
    b2 = reduce_relay(rb, 6, b1, yp, ym, fb1, fb2, gb1, gb2, y_plus, y_minus)

    arrive(pa_sib, pa.at[1, h])
    arrive(pa_fwd, pa.at[1, 1 - h])
    arrive(og_s, og_sib)
    back(og_sib, 1)

    repack(ra, a2, x, ga1, ga2, ya)
    a3 = reduce_start(ya, 3, yo, ha1, ha2, y_plus, y_minus)
    repack(rb, b2, y, gb1, gb2, xb)
    b3 = reduce_start(xb, 3, xo, hb1, hb2, x_plus, x_minus)
    wide_finish(nm_own, nm_w2)
    nm_s = send(nm_own, nm_sib, sibling)

    def down(s):
        lanes = slice(s * BLK, (s + 1) * BLK)
        pick = select_rows(64, BLK, lambda r: r + dp * 64)
        mine = dot(pick, act[:, lanes], ((1,), (1,))).astype(BF16)

        def one(k, carry):
            b = col_ref[2 * mp + s, k]
            seen = jnp.concatenate([tokens(og_own, b), tokens(og_sib, b)], axis=0)
            start = pl.multiple_of(k * BLK, BLK)
            dng_ref[s, :, pl.ds(start, BLK)] = dot(mine, seen, ((1,), (0,))).astype(BF16)
            return carry

        lax.fori_loop(0, KEPT, one, 0)

    a4 = reduce_relay(ya, 3, a3, yp, ym, ha1, ha2, ka1, ka2, y_plus, y_minus)
    b4 = reduce_relay(xb, 3, b3, xp, xm, hb1, hb2, kb1, kb2, x_plus, x_minus)
    down(0)

    def total(r, sems, at, g1, g2):
        arrive(sems[0], g1)
        arrive(sems[1], g2)
        sums = [r[at, j].astype(F32) + g1[j].astype(F32) + g2[j].astype(F32) for j in range(6)]
        return [
            jnp.concatenate(sums[3 * q : 3 * q + 3], axis=1).astype(BF16) for q in range(2)
        ]

    stacked = jnp.concatenate(total(ya, a4, y, ka1, ka2) + total(xb, b4, x, kb1, kb2), axis=0)
    order = select_rows(
        64,
        64,
        lambda r: lax.div(lax.rem(r, 16), 8) * 32
        + lax.rem(lax.div(r, 2), 2) * 16
        + lax.rem(lax.div(r, 4), 2) * 8
        + lax.div(r, 16) * 2
        + lax.rem(r, 2),
    )
    zs[...] = dot(order, stacked, ((1,), (0,))).astype(BF16).reshape(4, 16, PIECE)
    z_last = []
    for k in range(1, 4):
        to = lax.rem(z + k, 4)
        z_last.append(send(zs.at[to], zr.at[k - 1], device(z=to)))

    down(1)

    for k in range(3):
        arrive(z_last[k], zr.at[k])
    normed_grad = (
        zs[z].astype(F32) + zr[0].astype(F32) + zr[1].astype(F32) + zr[2].astype(F32)
    )
    scaled = normed_grad * gain16[...]
    unit_rows = unit16[...]
    pack[...] = inv16[:, 0:1] * (
        scaled - token_mean(scaled) - unit_rows * token_mean(scaled * unit_rows)
    )
    for p in range(PIECES):
        gin_ref[:, p * PIECE : (p + 1) * PIECE] = pack[2 * p : 2 * p + 2, :].astype(BF16)

    arrive(nm_s, nm_sib)

    for s in range(SLOTS):
        lanes = slice(s * BLK, (s + 1) * BLK)

        def grow_up(k, carry):
            b = row_ref[2 * mp + s, dp * 4 + k]
            picked = jnp.concatenate([tokens(nm_own, b), tokens(nm_sib, b)], axis=0)
            start = pl.multiple_of(k * BLK, BLK)
            upg_ref[s, pl.ds(start, BLK), :] = dot(picked, pg[:, lanes], ((0,), (0,))).astype(BF16)
            return carry

        lax.fori_loop(0, 4, grow_up, 0)

    for copy in started:
        copy.wait_send()


def local(
    inputs, out_grad, pre_act, norm_gain, up_weight, down_weight, row_blocks, col_blocks, counts
):
    vmem = pl.BlockSpec(memory_space=pltpu.VMEM)
    smem = pl.BlockSpec(memory_space=pltpu.SMEM)
    hbm = pl.BlockSpec(memory_space=pl.ANY)
    gathered = pltpu.VMEM((48, 4, 4, 16, 128), BF16)
    return pl.pallas_call(
        kernel,
        out_shape=(
            jax.ShapeDtypeStruct((2, FEATURES), BF16),
            jax.ShapeDtypeStruct((SLOTS, 1024, BLK), BF16),
            jax.ShapeDtypeStruct((SLOTS, 64, 4096), BF16),
        ),
        in_specs=[vmem, vmem, hbm, vmem, hbm, hbm, smem, smem, smem],
        out_specs=(vmem, vmem, vmem),
        scratch_shapes=[
            pltpu.VMEM((SLOTS, KEPT + 1, BLK, BLK), BF16),
            pltpu.VMEM((SLOTS, BLK, 4096), BF16),
            pltpu.VMEM((128, 512), BF16),
            pltpu.VMEM((2, 2, 128, 512), BF16),
            pltpu.VMEM((16, PIECE), F32),
            pltpu.VMEM((16, PIECE), F32),
            pltpu.VMEM((16, PIECE), F32),
            pltpu.VMEM((16, 128), F32),
            pltpu.VMEM((8, 16, PIECE), BF16),
            pltpu.VMEM((8, 16, PIECE), BF16),
            gathered, gathered, gathered, gathered,
            pltpu.VMEM((SLOTS, 256, BLK), F32),
            pltpu.VMEM((512, 512), BF16),
            pltpu.VMEM((512, 512), BF16),
            pltpu.VMEM((128, 512), BF16),
            pltpu.VMEM((128, 512), BF16),
        ]
        + [pltpu.VMEM((4, 12, 32, BLK), BF16)] * 2
        + [pltpu.VMEM((6, 32, BLK), BF16)] * 4
        + [pltpu.VMEM((12, 32, BLK), BF16)] * 4
        + [pltpu.VMEM((4, 6, 16, BLK), BF16)] * 2
        + [pltpu.VMEM((3, 16, BLK), BF16)] * 4
        + [pltpu.VMEM((6, 16, BLK), BF16)] * 4
        + [
            pltpu.VMEM((4, 16, PIECE), BF16),
            pltpu.VMEM((3, 16, PIECE), BF16),
            pltpu.SMEM((48,), jnp.int32),
            pltpu.SemaphoreType.DMA((4,)),
            pltpu.SemaphoreType.DMA((N_COPIES,)),
            pltpu.SemaphoreType.DMA((N_COPIES,)),
        ],
        compiler_params=pltpu.CompilerParams(
            collective_id=0, has_side_effects=True, vmem_limit_bytes=48 * 1024 * 1024
        ),
    )(
        inputs,
        out_grad,
        pre_act,
        norm_gain.reshape(1, FEATURES),
        up_weight.reshape(SLOTS, KEPT, BLK, BLK),
        down_weight,
        row_blocks,
        col_blocks,
        counts,
    )


def solution(mesh):
    placed = (
        P(("dp", "mp"), None),
        P(("dp", "mp"), None),
        P("dp", "mp"),
        P(),
        P("mp", None, None),
        P("mp", None, None),
        P(),
        P(),
        P(),
    )
    return jax.shard_map(
        local,
        mesh=mesh,
        in_specs=placed,
        out_specs=(P(("dp", "mp"), None), P("mp", "dp", None), P("mp", "dp", None)),
        check_vma=False,
    )
```

```python
import math

import jax
import jax.numpy as jnp
from jax import lax
from jax.experimental import pallas as pl
from jax.experimental.pallas import tpu as pltpu
from jax.sharding import PartitionSpec as P

EPS = 1e-06
F32 = jnp.float32
BF16 = jnp.bfloat16
PIECES = 8
PIECE = 768
BLK = 256
SLOTS = 2
KEPT = 16
FEATURES = 6144
LANES = 24
N_COPIES = 112


def dot(a, b, dims):
    return lax.dot_general(a, b, (dims, ((), ())), preferred_element_type=F32)


def select_rows(rows, columns, source_of):
    r = lax.broadcasted_iota(jnp.int32, (rows, columns), 0)
    c = lax.broadcasted_iota(jnp.int32, (rows, columns), 1)
    return (c == source_of(r)).astype(BF16)


def gelu_pair(z):
    a = math.sqrt(2.0 / math.pi)
    z2 = z * z
    t = jnp.tanh(a * z * (1.0 + 0.044715 * z2))
    half = 0.5 * (1.0 + t)
    slope = half + 0.5 * z * (1.0 - t * t) * (a * (1.0 + 3.0 * 0.044715 * z2))
    return z * half, slope


def kernel(
    x_hbm, og_hbm, pre_hbm, gain_hbm, up_hbm, dn_hbm, row_ref, col_ref, cnt_ref,
    gin_ref, upg_ref, dng_ref,
    x_ref, og_ref, gain_ref, up, dn, pre, pa,
    pack, gain16, unit16, inv16,
    raw_own, raw_oth, raw_nm,
    o_own, o_oth, t0, t1, t2, t3, n_own, n_sib,
    acc, act, pg, pg_z, pgb,
    ra, rb, ga, gb, ya, xb, ka, kb,
    zs, zr, pos,
    local_sem, send_sem, recv_sem,
):
    dp = lax.axis_index("dp")
    mp = lax.axis_index("mp")
    h, c = lax.div(dp, 2), lax.rem(dp, 2)
    z, x, y = lax.div(mp, 16), lax.rem(lax.div(mp, 4), 4), lax.rem(mp, 4)
    z8 = h * 4 + z

    def device(h=h, c=c, z=z, x=x, y=y):
        return {"dp": h * 2 + c, "mp": z * 16 + x * 4 + y}

    def around(at, by, n=4):
        return lax.rem(at + by + n, n)

    def z_device(at):
        return device(h=lax.div(at, 4), z=lax.rem(at, 4))

    x_peer = {d: device(x=around(x, d)) for d in (1, 2, 3)}
    y_peer = {d: device(y=around(y, d)) for d in (1, 2, 3)}
    z_plus, z_minus = z_device(around(z8, 1, 8)), z_device(around(z8, -1, 8))
    sibling = device(c=1 - c)
    partner = device(h=1 - h)

    started = []
    count = [0]

    def send(src, dst, target):
        k = count[0]
        count[0] += 1
        copy = pltpu.make_async_remote_copy(
            src_ref=src, dst_ref=dst, send_sem=send_sem.at[k], recv_sem=recv_sem.at[k],
            device_id=target, device_id_type=pl.DeviceIdType.MESH,
        )
        copy.start()
        started.append(copy)
        return k

    def arrive(k, dst):
        pltpu.make_async_remote_copy(
            src_ref=dst, dst_ref=dst, send_sem=send_sem.at[k], recv_sem=recv_sem.at[k],
            device_id=sibling, device_id_type=pl.DeviceIdType.MESH,
        ).wait_recv()

    def fetch(src, dst, k):
        copy = pltpu.make_async_copy(src, dst, local_sem.at[k])
        copy.start()
        return copy

    og_copy = fetch(og_hbm, og_ref, 0)
    x_copy = fetch(x_hbm, x_ref, 1)
    gain_copy = fetch(gain_hbm, gain_ref, 2)
    pre_copy = fetch(pre_hbm, pre, 3)

    barrier = pltpu.get_barrier_semaphore()
    greeted = [z_device(around(z8, k, 8)) for k in range(1, 8)]
    greeted += list(x_peer.values()) + list(y_peer.values()) + [sibling]
    for target in greeted:
        pl.semaphore_signal(
            barrier, inc=1, device_id=target, device_id_type=pl.DeviceIdType.MESH
        )

    weight_copies = [fetch(dn_hbm, dn, 4)]
    weight_copies += [fetch(up_hbm.at[s], up.at[s, pl.ds(0, KEPT)], 5 + s) for s in range(SLOTS)]

    og_copy.wait()
    for p in range(PIECES):
        pack[2 * p : 2 * p + 2, :] = og_ref[:, p * PIECE : (p + 1) * PIECE].astype(F32)
    raw_own[z] = pack[...].astype(BF16)
    x_copy.wait()
    gain_copy.wait()
    for p in range(PIECES):
        pack[2 * p : 2 * p + 2, :] = x_ref[:, p * PIECE : (p + 1) * PIECE].astype(F32)
        gain16[2 * p : 2 * p + 2, :] = jnp.broadcast_to(
            gain_ref[:, p * PIECE : (p + 1) * PIECE], (2, PIECE)
        )
    first = lax.rem(lax.broadcasted_iota(jnp.int32, (16, 1), 0), 2) == 0

    def token_mean(values):
        rows = jnp.sum(values, axis=1, keepdims=True)
        total0 = jnp.sum(jnp.where(first, rows, 0.0), axis=0, keepdims=True)
        total1 = jnp.sum(jnp.where(first, 0.0, rows), axis=0, keepdims=True)
        return jnp.where(first, total0, total1) * (1.0 / FEATURES)

    widened = pack[...]
    centred = widened - token_mean(widened)
    inv_std = lax.rsqrt(token_mean(centred * centred) + EPS)
    unit_rows = centred * inv_std
    unit16[...] = unit_rows
    inv16[...] = jnp.broadcast_to(inv_std, (16, 128))
    raw_nm[y, x] = (unit_rows * gain16[...]).astype(BF16)

    pl.semaphore_wait(barrier, len(greeted))

    own_z = [
        (d, send(raw_own.at[z], raw_own.at[z], device(z=around(z, d)))) for d in (1, 2, 3)
    ]
    nm_x = [(d, send(raw_nm.at[y, x], raw_nm.at[y, x], x_peer[d])) for d in (1, 2, 3)]
    oth_z = [
        (d, send(raw_own.at[z], raw_oth.at[z], device(h=1 - h, z=around(z, d)))) for d in range(4)
    ]

    pre_copy.wait()
    order = select_rows(
        128, 128, lambda r: lax.div(lax.rem(r, 8), 2) * 32 + lax.div(r, 8) * 2 + lax.rem(r, 2)
    )
    pa[0] = dot(order, pre[...], ((1,), (0,))).astype(BF16)
    pa_sib = send(pa.at[0], pa.at[2], sibling)

    def place(raw, tiles, arrivals):
        for d, sem in arrivals:
            arrive(sem, raw.at[around(z, -d)])
        order = select_rows(
            64,
            64,
            lambda r: lax.div(lax.rem(r, 8), 2) * 16
            + lax.div(lax.rem(r, 16), 8) * 8
            + lax.div(r, 16) * 2
            + lax.rem(r, 2),
        )
        out = dot(order, raw[...].reshape(64, PIECE), ((1,), (0,))).astype(BF16)
        for p in range(4):
            for q in range(6):
                tiles[p * 6 + q, x, y] = out[16 * p : 16 * p + 16, 128 * q : 128 * q + 128]

    lane_a, lane_b = pl.ds(0, 12), pl.ds(12, 12)

    def narrow_send(o):
        a, b = o.at[lane_a, x, y], o.at[lane_b, x, y]
        return [(d, send(a, a, x_peer[d]), send(b, b, y_peer[d])) for d in (1, 3, 2)]

    def column_send(o, at_x, at_y):
        a, b = o.at[lane_a, at_x, y], o.at[lane_b, x, at_y]
        return [(d, send(a, a, y_peer[d]), send(b, b, x_peer[d])) for d in (1, 3, 2)]

    def narrow_wait(o, sem):
        d, sem_a, sem_b = sem
        arrive(sem_a, o.at[lane_a, around(x, -d), y])
        arrive(sem_b, o.at[lane_b, x, around(y, -d)])

    place(raw_own, o_own, own_z)
    own_n = narrow_send(o_own)
    own_w = [(0, column_send(o_own, x, y))]
    pa_part = send(pa.at[0], pa.at[1], partner)
    for d, sem in nm_x:
        arrive(sem, raw_nm.at[y, around(x, -d)])
    nm_y = [(d, send(raw_nm.at[y], raw_nm.at[y], y_peer[d])) for d in (1, 2, 3)]
    place(raw_oth, o_oth, oth_z)
    for sem in own_n:
        narrow_wait(o_own, sem)
        own_w.append((sem[0], column_send(o_own, around(x, -sem[0]), around(y, -sem[0]))))
    oth_n = narrow_send(o_oth)

    for d, sem in nm_y:
        arrive(sem, raw_nm.at[around(y, -d)])
    order = select_rows(
        256,
        256,
        lambda r: lax.div(lax.rem(r, 8), 2) * 64
        + lax.div(lax.rem(r, 32), 8) * 16
        + lax.div(r, 32) * 2
        + lax.rem(r, 2),
    )
    out = dot(order, raw_nm[...].reshape(256, PIECE), ((1,), (0,))).astype(BF16)
    for p in range(PIECES):
        for q in range(6):
            n_own[z8, p * 6 + q] = out[32 * p : 32 * p + 32, 128 * q : 128 * q + 128]

    steps = [(0, 0), (0, 1), (1, 0), (1, 1), (2, 0), (2, 1), (3, 0)]
    halves = (pl.ds(0, 24), pl.ds(24, 24))
    nm_sems = {}

    def ring_send(n):
        far, half = steps[n]
        plus = n_own.at[around(z8, -far, 8), halves[half]]
        minus = n_own.at[around(z8, far, 8), halves[1 - half]]
        nm_sems[n] = (send(plus, plus, z_plus), send(minus, minus, z_minus))

    nm_sib = []

    def to_sibling(at):
        nm_sib.append((at, send(n_own.at[at], n_sib.at[at], sibling)))

    def ring_poll(n):
        far, half = steps[n]
        arrive(nm_sems[n][0], n_own.at[around(z8, -far - 1, 8), halves[half]])
        arrive(nm_sems[n][1], n_own.at[around(z8, far + 1, 8), halves[1 - half]])
        if n + 2 < len(steps):
            ring_send(n + 2)
        if half == 1:
            to_sibling(around(z8, far + 1, 8))
            to_sibling(around(z8, -far - 1, 8))
        if n == 6:
            to_sibling(around(z8, 4, 8))

    ring_send(0)
    ring_send(1)
    to_sibling(z8)

    for s in range(SLOTS):
        up[s, KEPT] = jnp.zeros((BLK, BLK), BF16)

    def locate(b, carry):
        for s in range(SLOTS):
            found = jnp.int32(KEPT)
            for k in range(KEPT):
                found = jnp.where(row_ref[k, 2 * mp + s] == b, k, found)
            pos[s * 24 + b] = found
        return carry

    lax.fori_loop(0, 24, locate, 0)
    for sem in oth_n:
        narrow_wait(o_oth, sem)
    arrive(pa_part, pa.at[1])
    pa_fwd = send(pa.at[1], pa.at[3], sibling)
    for copy in weight_copies:
        copy.wait()
    ring_poll(0)
    for far, sems in own_w:
        for d, sem_a, sem_b in sems:
            arrive(sem_a, o_own.at[lane_a, around(x, -far), around(y, -d)])
            arrive(sem_b, o_own.at[lane_b, around(x, -d), around(y, -far)])
    a, b = o_oth.at[lane_a, :, y], o_oth.at[lane_b, x]
    oth_w = [(d, send(a, a, y_peer[d]), send(b, b, x_peer[d])) for d in (1, 3, 2)]

    def unpack(o, t):
        def one(k, carry):
            rows = o[k].astype(F32).reshape(16, 2, 8, 128)
            t[k] = rows[:, 0].reshape(128, 128).astype(BF16)
            t[LANES + k] = rows[:, 1].reshape(128, 128).astype(BF16)
            return carry

        lax.fori_loop(0, LANES, one, 0)

    unpack(o_own, t0)
    t_sib0 = send(t0, t2, sibling)

    live = [s < cnt_ref[mp] for s in range(SLOTS)]

    def tokens(t, b):
        return jnp.concatenate([t[2 * b], t[2 * b + 1]], axis=-1)

    def back(groups):
        rows = 128 * len(groups)
        for s in range(SLOTS):

            def grow(k, carry):
                parts = []
                for j in range(4):
                    b = col_ref[4 * k + j, 2 * mp + s]
                    parts.append(jnp.concatenate([tokens(t, b) for t in groups.values()], axis=0))
                start = pl.multiple_of(k * 1024, 1024)
                term = dot(
                    jnp.concatenate(parts, axis=1), dn[s, :, pl.ds(start, 1024)], ((1,), (1,))
                )

                @pl.when(k == 0)
                def _():
                    acc[s, 0:rows] = term

                @pl.when(k > 0)
                def _():
                    acc[s, 0:rows] += term

                return carry

            lax.fori_loop(0, KEPT // 4, grow, 0)

        def derive(j, carry):
            at = pl.ds(pl.multiple_of(j * 16, 16), 16)
            for n, g in enumerate(groups):
                for s in range(SLOTS):
                    lanes = slice(s * BLK, (s + 1) * BLK)
                    value, slope = gelu_pair(pa[g, at, lanes].astype(F32))
                    grad = acc[s, pl.ds(pl.multiple_of(n * 128 + j * 16, 16), 16), :] * slope
                    pg[g, at, lanes] = jnp.where(live[s], grad, 0.0).astype(BF16)
                    act[g, at, lanes] = jnp.where(live[s], value, 0.0).astype(BF16)
            return carry

        lax.fori_loop(0, 8, derive, 0)

    back({0: t0})

    order = select_rows(
        128, 128, lambda r: lax.div(lax.rem(r, 32), 8) * 32 + lax.div(r, 32) * 8 + lax.rem(r, 8)
    )
    pgb[...] = dot(order, pg[0], ((1,), (0,))).astype(BF16)

    def terms(source, out, base, first):
        def one(b, carry):
            weights = [up[s, pos[s * 24 + base + b]] for s in range(SLOTS)]
            term = dot(source, jnp.concatenate(weights, axis=1), ((1,), (1,))).astype(BF16)
            for q in range(4):
                out[q, b] = term[32 * q : 32 * q + 32]
            return carry

        lax.fori_loop(first, first + 6, one, 0)

    def reduce_send(r, at, g, peers, blocks):
        return [
            (d, send(r.at[around(at, d), blocks], g.at[d - 1, blocks], peers[d])) for d in (2, 1, 3)
        ]

    part0, part1 = pl.ds(0, 6), pl.ds(6, 6)
    terms(pg[0], ra, 0, 0)
    a1 = reduce_send(ra, x, ga, x_peer, part0)
    terms(pgb[...], rb, 12, 0)
    b1 = reduce_send(rb, y, gb, y_peer, part0)
    terms(pg[0], ra, 0, 6)
    a2 = reduce_send(ra, x, ga, x_peer, part1)
    terms(pgb[...], rb, 12, 6)
    b2 = reduce_send(rb, y, gb, y_peer, part1)
    ring_poll(1)
    ring_poll(2)
    for d, sem_a, sem_b in oth_w:
        arrive(sem_a, o_oth.at[lane_a, :, around(y, -d)])
        arrive(sem_b, o_oth.at[lane_b, around(x, -d)])
    unpack(o_oth, t1)
    t_sib1 = send(t1, t3, sibling)
    ring_poll(3)
    arrive(pa_sib, pa.at[2])
    arrive(pa_fwd, pa.at[3])
    arrive(t_sib0, t2)

    def collect(r, at, g, groups, blocks):
        for sems, part in groups:
            for d, sem in sems:
                arrive(sem, g.at[d - 1, part])
        return [
            r[at, j].astype(F32) + g[0, j].astype(F32) + g[1, j].astype(F32) + g[2, j].astype(F32)
            for j in range(blocks)
        ]

    def repack(sums, out):
        for j in range(6):
            for q in range(4):
                rows = slice(8 * q, 8 * q + 8)
                both = jnp.concatenate([sums[j][rows], sums[6 + j][rows]], axis=0)
                out[q, j] = both.astype(BF16)

    whole = pl.ds(0, 6)
    repack(collect(ra, x, ga, [(a1, part0), (a2, part1)], 12), ya)
    a3 = reduce_send(ya, y, ka, y_peer, whole)
    repack(collect(rb, y, gb, [(b1, part0), (b2, part1)], 12), xb)
    b3 = reduce_send(xb, x, kb, x_peer, whole)
    ring_poll(4)
    arrive(t_sib1, t3)
    back({1: t1, 2: t2, 3: t3})

    def total(r, at, g, sems):
        sums = collect(r, at, g, [(sems, whole)], 6)
        return [jnp.concatenate(sums[3 * q : 3 * q + 3], axis=1).astype(BF16) for q in range(2)]

    stacked = jnp.concatenate(total(ya, y, ka, a3) + total(xb, x, kb, b3), axis=0)
    order = select_rows(
        64,
        64,
        lambda r: lax.div(lax.rem(r, 16), 8) * 32
        + lax.rem(lax.div(r, 2), 2) * 16
        + lax.rem(lax.div(r, 4), 2) * 8
        + lax.div(r, 16) * 2
        + lax.rem(r, 2),
    )
    zs[...] = dot(order, stacked, ((1,), (0,))).astype(BF16).reshape(4, 16, PIECE)
    z_last = []
    for d in (3, 2, 1):
        to = around(z, d)
        z_last.append((d, send(zs.at[to], zr.at[d - 1], device(z=to))))
    ring_poll(5)

    def down(s):
        lanes = slice(s * BLK, (s + 1) * BLK)
        pick = select_rows(64, BLK, lambda r: r + dp * 64)
        mine = dot(pick, act[:, :, lanes].reshape(512, BLK), ((1,), (1,))).astype(BF16)

        def one(k, carry):
            b = col_ref[k, 2 * mp + s]
            seen = jnp.concatenate([tokens(t, b) for t in (t0, t1, t2, t3)], axis=0)
            start = pl.multiple_of(k * BLK, BLK)
            dng_ref[s, :, pl.ds(start, BLK)] = dot(mine, seen, ((1,), (0,))).astype(BF16)
            return carry

        lax.fori_loop(0, KEPT, one, 0)

    down(0)
    ring_poll(6)
    down(1)

    for d, sem in z_last:
        arrive(sem, zr.at[d - 1])
    normed_grad = (
        zs[z].astype(F32) + zr[0].astype(F32) + zr[1].astype(F32) + zr[2].astype(F32)
    )
    scaled = normed_grad * gain16[...]
    unit_rows = unit16[...]
    pack[...] = inv16[:, 0:1] * (
        scaled - token_mean(scaled) - unit_rows * token_mean(scaled * unit_rows)
    )
    for p in range(PIECES):
        gin_ref[:, p * PIECE : (p + 1) * PIECE] = pack[2 * p : 2 * p + 2, :].astype(BF16)

    def z_order(r):
        at = lax.div(r, 32)
        near = lax.rem(lax.div(at, 4) + h, 2)
        return near * 128 + lax.div(lax.rem(r, 32), 2) * 8 + lax.rem(at, 4) * 2 + lax.rem(r, 2)

    order = select_rows(256, 256, z_order)
    for core in range(2):
        both = pg[2 * core : 2 * core + 2].reshape(256, 2 * BLK)
        pg_z[core] = dot(order, both, ((1,), (0,))).astype(BF16)

    for at, sem in nm_sib:
        arrive(sem, n_sib.at[at])

    for s in range(SLOTS):
        lanes = slice(s * BLK, (s + 1) * BLK)

        def grow_up(k, carry):
            b = row_ref[dp * 4 + k, 2 * mp + s]
            picked = jnp.concatenate(
                [
                    jnp.concatenate([n[:, 2 * b], n[:, 2 * b + 1]], axis=-1).reshape(BLK, BLK)
                    for n in (n_own, n_sib)
                ],
                axis=0,
            )
            grads = pg_z[:, :, lanes].reshape(512, BLK)
            start = pl.multiple_of(k * BLK, BLK)
            upg_ref[s, pl.ds(start, BLK), :] = dot(picked, grads, ((0,), (0,))).astype(BF16)
            return carry

        lax.fori_loop(0, 4, grow_up, 0)

    for copy in started:
        copy.wait_send()


def local(
    inputs, out_grad, pre_act, norm_gain, up_weight, down_weight, row_blocks, col_blocks, counts
):
    vmem = pl.BlockSpec(memory_space=pltpu.VMEM)
    smem = pl.BlockSpec(memory_space=pltpu.SMEM)
    hbm = pl.BlockSpec(memory_space=pltpu.HBM)
    return pl.pallas_call(
        kernel,
        out_shape=(
            jax.ShapeDtypeStruct((2, FEATURES), BF16),
            jax.ShapeDtypeStruct((SLOTS, 1024, BLK), BF16),
            jax.ShapeDtypeStruct((SLOTS, 64, 4096), BF16),
        ),
        in_specs=[hbm, hbm, hbm, hbm, hbm, hbm, smem, smem, smem],
        out_specs=(vmem, vmem, vmem),
        scratch_shapes=[
            pltpu.VMEM((2, FEATURES), BF16),
            pltpu.VMEM((2, FEATURES), BF16),
            pltpu.VMEM((1, FEATURES), F32),
            pltpu.VMEM((SLOTS, KEPT + 1, BLK, BLK), BF16),
            pltpu.VMEM((SLOTS, BLK, 4096), BF16),
            pltpu.VMEM((128, 512), BF16),
            pltpu.VMEM((4, 128, 512), BF16),
            pltpu.VMEM((16, PIECE), F32),
            pltpu.VMEM((16, PIECE), F32),
            pltpu.VMEM((16, PIECE), F32),
            pltpu.VMEM((16, 128), F32),
            pltpu.VMEM((4, 16, PIECE), BF16),
            pltpu.VMEM((4, 16, PIECE), BF16),
            pltpu.VMEM((4, 4, 16, PIECE), BF16),
        ]
        + [pltpu.VMEM((LANES, 4, 4, 16, 128), BF16)] * 2
        + [pltpu.VMEM((2 * LANES, 128, 128), BF16)] * 4
        + [pltpu.VMEM((8, 2 * LANES, 32, 128), BF16)] * 2
        + [
            pltpu.VMEM((SLOTS, 384, BLK), F32),
            pltpu.VMEM((4, 128, 512), BF16),
            pltpu.VMEM((4, 128, 512), BF16),
            pltpu.VMEM((2, 256, 512), BF16),
            pltpu.VMEM((128, 512), BF16),
        ]
        + [pltpu.VMEM((4, 12, 32, BLK), BF16)] * 2
        + [pltpu.VMEM((3, 12, 32, BLK), BF16)] * 2
        + [pltpu.VMEM((4, 6, 16, BLK), BF16)] * 2
        + [pltpu.VMEM((3, 6, 16, BLK), BF16)] * 2
        + [
            pltpu.VMEM((4, 16, PIECE), BF16),
            pltpu.VMEM((3, 16, PIECE), BF16),
            pltpu.SMEM((48,), jnp.int32),
            pltpu.SemaphoreType.DMA((7,)),
            pltpu.SemaphoreType.DMA((N_COPIES,)),
            pltpu.SemaphoreType.DMA((N_COPIES,)),
        ],
        compiler_params=pltpu.CompilerParams(
            collective_id=0, has_side_effects=True, vmem_limit_bytes=48 * 1024 * 1024
        ),
    )(
        inputs,
        out_grad,
        pre_act,
        norm_gain.reshape(1, FEATURES),
        up_weight.reshape(SLOTS, KEPT, BLK, BLK),
        down_weight,
        row_blocks.T,
        col_blocks.T,
        counts,
    )


def solution(mesh):
    placed = (
        P(("dp", "mp"), None),
        P(("dp", "mp"), None),
        P("dp", "mp"),
        P(),
        P("mp", None, None),
        P("mp", None, None),
        P(),
        P(),
        P(),
    )
    return jax.shard_map(
        local,
        mesh=mesh,
        in_specs=placed,
        out_specs=(P(("dp", "mp"), None), P("mp", "dp", None), P("mp", "dp", None)),
        check_vma=False,
    )
```

```python
import math

import jax
import jax.numpy as jnp
from jax import lax
from jax.experimental import pallas as pl
from jax.experimental.pallas import tpu as pltpu
from jax.sharding import PartitionSpec as P

EPS = 1e-06
F32 = jnp.float32
BF16 = jnp.bfloat16
PIECES = 8
PIECE = 768
BLK = 256
SLOTS = 2
KEPT = 16
FEATURES = 6144
LANES = 24
N_COPIES = 112


def dot(a, b, dims):
    return lax.dot_general(a, b, (dims, ((), ())), preferred_element_type=F32)


def select_rows(rows, columns, source_of):
    r = lax.broadcasted_iota(jnp.int32, (rows, columns), 0)
    c = lax.broadcasted_iota(jnp.int32, (rows, columns), 1)
    return (c == source_of(r)).astype(BF16)


def gelu_pair(z):
    a = math.sqrt(2.0 / math.pi)
    z2 = z * z
    t = jnp.tanh(a * z * (1.0 + 0.044715 * z2))
    half = 0.5 * (1.0 + t)
    slope = half + 0.5 * z * (1.0 - t * t) * (a * (1.0 + 3.0 * 0.044715 * z2))
    return z * half, slope


def kernel(
    x_hbm, og_hbm, pre_hbm, gain_hbm, up_hbm, dn_hbm, row_ref, col_ref, cnt_ref,
    gin_ref, upg_ref, dng_ref,
    x_ref, og_ref, gain_ref, up, dn, pre, pa,
    pack, gain16, unit16, inv16,
    raw_own, raw_oth, raw_nm,
    o_own, o_oth, t0, t1, t2, t3, n_own, n_sib,
    acc, act, pg, pg_z, pgb,
    ra, rb, ga, gb, ya, xb, ka, kb,
    zs, zr, pos,
    local_sem, send_sem, recv_sem,
):
    dp = lax.axis_index("dp")
    mp = lax.axis_index("mp")
    h, c = lax.div(dp, 2), lax.rem(dp, 2)
    z, x, y = lax.div(mp, 16), lax.rem(lax.div(mp, 4), 4), lax.rem(mp, 4)
    z8 = h * 4 + z

    def device(h=h, c=c, z=z, x=x, y=y):
        return {"dp": h * 2 + c, "mp": z * 16 + x * 4 + y}

    def around(at, by, n=4):
        return lax.rem(at + by + n, n)

    def z_device(at):
        return device(h=lax.div(at, 4), z=lax.rem(at, 4))

    x_peer = {d: device(x=around(x, d)) for d in (1, 2, 3)}
    y_peer = {d: device(y=around(y, d)) for d in (1, 2, 3)}
    z_plus, z_minus = z_device(around(z8, 1, 8)), z_device(around(z8, -1, 8))
    sibling = device(c=1 - c)
    partner = device(h=1 - h)

    started = []
    count = [0]

    def send(src, dst, target):
        k = count[0]
        count[0] += 1
        copy = pltpu.make_async_remote_copy(
            src_ref=src, dst_ref=dst, send_sem=send_sem.at[k], recv_sem=recv_sem.at[k],
            device_id=target, device_id_type=pl.DeviceIdType.MESH,
        )
        copy.start()
        started.append(copy)
        return k

    def arrive(k, dst):
        pltpu.make_async_remote_copy(
            src_ref=dst, dst_ref=dst, send_sem=send_sem.at[k], recv_sem=recv_sem.at[k],
            device_id=sibling, device_id_type=pl.DeviceIdType.MESH,
        ).wait_recv()

    def fetch(src, dst, k):
        copy = pltpu.make_async_copy(src, dst, local_sem.at[k])
        copy.start()
        return copy

    og_copy = fetch(og_hbm, og_ref, 0)
    x_copy = fetch(x_hbm, x_ref, 1)
    gain_copy = fetch(gain_hbm, gain_ref, 2)
    pre_copy = fetch(pre_hbm, pre, 3)

    barrier = pltpu.get_barrier_semaphore()
    greeted = [z_device(around(z8, k, 8)) for k in range(1, 8)]
    greeted += list(x_peer.values()) + list(y_peer.values()) + [sibling]
    for target in greeted:
        pl.semaphore_signal(
            barrier, inc=1, device_id=target, device_id_type=pl.DeviceIdType.MESH
        )

    weight_copies = [fetch(dn_hbm, dn, 4)]
    weight_copies += [fetch(up_hbm.at[s], up.at[s, pl.ds(0, KEPT)], 5 + s) for s in range(SLOTS)]

    og_copy.wait()
    for p in range(PIECES):
        pack[2 * p : 2 * p + 2, :] = og_ref[:, p * PIECE : (p + 1) * PIECE].astype(F32)
    raw_own[z] = pack[...].astype(BF16)
    x_copy.wait()
    gain_copy.wait()
    for p in range(PIECES):
        pack[2 * p : 2 * p + 2, :] = x_ref[:, p * PIECE : (p + 1) * PIECE].astype(F32)
        gain16[2 * p : 2 * p + 2, :] = jnp.broadcast_to(
            gain_ref[:, p * PIECE : (p + 1) * PIECE], (2, PIECE)
        )
    first = lax.rem(lax.broadcasted_iota(jnp.int32, (16, 1), 0), 2) == 0

    def token_mean(values):
        rows = jnp.sum(values, axis=1, keepdims=True)
        total0 = jnp.sum(jnp.where(first, rows, 0.0), axis=0, keepdims=True)
        total1 = jnp.sum(jnp.where(first, 0.0, rows), axis=0, keepdims=True)
        return jnp.where(first, total0, total1) * (1.0 / FEATURES)

    widened = pack[...]
    centred = widened - token_mean(widened)
    inv_std = lax.rsqrt(token_mean(centred * centred) + EPS)
    unit_rows = centred * inv_std
    unit16[...] = unit_rows
    inv16[...] = jnp.broadcast_to(inv_std, (16, 128))
    raw_nm[y, x] = (unit_rows * gain16[...]).astype(BF16)

    pl.semaphore_wait(barrier, len(greeted))

    own_z = [
        (d, send(raw_own.at[z], raw_own.at[z], device(z=around(z, d)))) for d in (1, 2, 3)
    ]
    cut_a, cut_b = pl.ds(0, PIECE // 2), pl.ds(PIECE // 2, PIECE // 2)
    a, b = raw_nm.at[y, x, :, cut_a], raw_nm.at[y, x, :, cut_b]
    nm_1 = [(d, send(a, a, x_peer[d]), send(b, b, y_peer[d])) for d in (1, 3, 2)]

    def place(raw, tiles, arrivals):
        for d, sem in arrivals:
            arrive(sem, raw.at[around(z, -d)])
        order = select_rows(
            64,
            64,
            lambda r: lax.div(lax.rem(r, 8), 2) * 16
            + lax.div(lax.rem(r, 16), 8) * 8
            + lax.div(r, 16) * 2
            + lax.rem(r, 2),
        )
        out = dot(order, raw[...].reshape(64, PIECE), ((1,), (0,))).astype(BF16)
        for p in range(4):
            for q in range(6):
                tiles[p * 6 + q, x, y] = out[16 * p : 16 * p + 16, 128 * q : 128 * q + 128]

    lane_a, lane_b = pl.ds(0, 12), pl.ds(12, 12)

    def narrow_send(o):
        a, b = o.at[lane_a, x, y], o.at[lane_b, x, y]
        return [(d, send(a, a, x_peer[d]), send(b, b, y_peer[d])) for d in (1, 3, 2)]

    def column_send(o, at_x, at_y):
        a, b = o.at[lane_a, at_x, y], o.at[lane_b, x, at_y]
        return [(d, send(a, a, y_peer[d]), send(b, b, x_peer[d])) for d in (1, 3, 2)]

    def narrow_wait(o, sem):
        d, sem_a, sem_b = sem
        arrive(sem_a, o.at[lane_a, around(x, -d), y])
        arrive(sem_b, o.at[lane_b, x, around(y, -d)])

    place(raw_own, o_own, own_z)
    own_n = narrow_send(o_own)
    own_w = [(0, column_send(o_own, x, y))]
    oth_z = [
        (d, send(raw_own.at[z], raw_oth.at[z], device(h=1 - h, z=around(z, d)))) for d in range(4)
    ]
    for d, sem_a, sem_b in nm_1:
        arrive(sem_a, raw_nm.at[y, around(x, -d), :, cut_a])
        arrive(sem_b, raw_nm.at[around(y, -d), x, :, cut_b])
    a, b = raw_nm.at[y, :, :, cut_a], raw_nm.at[:, x, :, cut_b]
    nm_2 = [(d, send(a, a, y_peer[d]), send(b, b, x_peer[d])) for d in (1, 3, 2)]

    pre_copy.wait()
    order = select_rows(
        128, 128, lambda r: lax.div(lax.rem(r, 8), 2) * 32 + lax.div(r, 8) * 2 + lax.rem(r, 2)
    )
    pa[0] = dot(order, pre[...], ((1,), (0,))).astype(BF16)
    pa_part = send(pa.at[0], pa.at[1], partner)
    pa_sib = send(pa.at[0], pa.at[2], sibling)

    for s in range(SLOTS):
        up[s, KEPT] = jnp.zeros((BLK, BLK), BF16)

    def locate(b, carry):
        for s in range(SLOTS):
            found = jnp.int32(KEPT)
            for k in range(KEPT):
                found = jnp.where(row_ref[k, 2 * mp + s] == b, k, found)
            pos[s * 24 + b] = found
        return carry

    lax.fori_loop(0, 24, locate, 0)
    for sem in own_n:
        narrow_wait(o_own, sem)
        own_w.append((sem[0], column_send(o_own, around(x, -sem[0]), around(y, -sem[0]))))

    for d, sem_a, sem_b in nm_2:
        arrive(sem_a, raw_nm.at[around(y, -d), :, :, cut_a])
        arrive(sem_b, raw_nm.at[:, around(x, -d), :, cut_b])
    order = select_rows(
        256,
        256,
        lambda r: lax.div(lax.rem(r, 8), 2) * 64
        + lax.div(lax.rem(r, 32), 8) * 16
        + lax.div(r, 32) * 2
        + lax.rem(r, 2),
    )
    out = dot(order, raw_nm[...].reshape(256, PIECE), ((1,), (0,))).astype(BF16)
    for p in range(PIECES):
        for q in range(6):
            n_own[z8, p * 6 + q] = out[32 * p : 32 * p + 32, 128 * q : 128 * q + 128]

    steps = [(0, 0), (0, 1), (1, 0), (1, 1), (2, 0), (2, 1), (3, 0)]
    halves = (pl.ds(0, 24), pl.ds(24, 24))
    nm_sems = {}

    def ring_send(n):
        far, half = steps[n]
        plus = n_own.at[around(z8, -far, 8), halves[half]]
        minus = n_own.at[around(z8, far, 8), halves[1 - half]]
        nm_sems[n] = (send(plus, plus, z_plus), send(minus, minus, z_minus))

    nm_sib = []

    def to_sibling(at):
        nm_sib.append((at, send(n_own.at[at], n_sib.at[at], sibling)))

    def ring_poll(n):
        far, half = steps[n]
        arrive(nm_sems[n][0], n_own.at[around(z8, -far - 1, 8), halves[half]])
        arrive(nm_sems[n][1], n_own.at[around(z8, far + 1, 8), halves[1 - half]])
        if n + 2 < len(steps):
            ring_send(n + 2)
        if half == 1:
            to_sibling(around(z8, far + 1, 8))
            to_sibling(around(z8, -far - 1, 8))
        if n == 6:
            to_sibling(around(z8, 4, 8))

    ring_send(0)
    ring_send(1)
    to_sibling(z8)

    place(raw_oth, o_oth, oth_z)
    oth_n = narrow_send(o_oth)
    for copy in weight_copies:
        copy.wait()
    for far, sems in own_w:
        for d, sem_a, sem_b in sems:
            arrive(sem_a, o_own.at[lane_a, around(x, -far), around(y, -d)])
            arrive(sem_b, o_own.at[lane_b, around(x, -d), around(y, -far)])
    for sem in oth_n:
        narrow_wait(o_oth, sem)

    def wide_send(o, lanes_a, lanes_b, from_x, from_y, d):
        a, b = o.at[lanes_a, :, from_y], o.at[lanes_b, from_x]
        return send(a, a, y_peer[d]), send(b, b, x_peer[d])

    def wide_wait(o, lanes_a, lanes_b, sems, d):
        arrive(sems[0], o.at[lanes_a, :, around(y, -d)])
        arrive(sems[1], o.at[lanes_b, around(x, -d)])

    quarter = [pl.ds(6 * k, 6) for k in range(4)]
    oth_w = {d: wide_send(o_oth, lane_a, lane_b, x, y, d) for d in (1, 3)}

    def oth_relay():
        for d, qa, qb in ((1, quarter[0], quarter[2]), (3, quarter[1], quarter[3])):
            wide_wait(o_oth, lane_a, lane_b, oth_w[d], d)
            oth_w[d + 10] = wide_send(o_oth, qa, qb, around(x, -d), around(y, -d), d)

    def oth_finish():
        wide_wait(o_oth, quarter[0], quarter[2], oth_w[11], 2)
        wide_wait(o_oth, quarter[1], quarter[3], oth_w[13], 2)

    ring_poll(0)

    def unpack(o, t):
        def one(k, carry):
            rows = o[k].astype(F32).reshape(16, 2, 8, 128)
            t[k] = rows[:, 0].reshape(128, 128).astype(BF16)
            t[LANES + k] = rows[:, 1].reshape(128, 128).astype(BF16)
            return carry

        lax.fori_loop(0, LANES, one, 0)

    unpack(o_own, t0)
    t_sib0 = send(t0, t2, sibling)

    live = [s < cnt_ref[mp] for s in range(SLOTS)]

    def tokens(t, b):
        return jnp.concatenate([t[2 * b], t[2 * b + 1]], axis=-1)

    def back(groups, between=lambda: None):
        rows = 128 * len(groups)
        for s in range(SLOTS):

            def grow(k, carry):
                parts = []
                for j in range(4):
                    b = col_ref[4 * k + j, 2 * mp + s]
                    parts.append(jnp.concatenate([tokens(t, b) for t in groups.values()], axis=0))
                start = pl.multiple_of(k * 1024, 1024)
                term = dot(
                    jnp.concatenate(parts, axis=1), dn[s, :, pl.ds(start, 1024)], ((1,), (1,))
                )

                @pl.when(k == 0)
                def _():
                    acc[s, 0:rows] = term

                @pl.when(k > 0)
                def _():
                    acc[s, 0:rows] += term

                return carry

            lax.fori_loop(0, KEPT // 4, grow, 0)
            if s == 0:
                between()

        def derive(j, carry):
            at = pl.ds(pl.multiple_of(j * 16, 16), 16)
            for n, g in enumerate(groups):
                for s in range(SLOTS):
                    lanes = slice(s * BLK, (s + 1) * BLK)
                    value, slope = gelu_pair(pa[g, at, lanes].astype(F32))
                    grad = acc[s, pl.ds(pl.multiple_of(n * 128 + j * 16, 16), 16), :] * slope
                    pg[g, at, lanes] = jnp.where(live[s], grad, 0.0).astype(BF16)
                    act[g, at, lanes] = jnp.where(live[s], value, 0.0).astype(BF16)
            return carry

        lax.fori_loop(0, 8, derive, 0)

    back({0: t0}, lambda: ring_poll(1))

    order = select_rows(
        128, 128, lambda r: lax.div(lax.rem(r, 32), 8) * 32 + lax.div(r, 32) * 8 + lax.rem(r, 8)
    )
    pgb[...] = dot(order, pg[0], ((1,), (0,))).astype(BF16)

    def terms(source, out, base, first):
        def one(b, carry):
            weights = [up[s, pos[s * 24 + base + b]] for s in range(SLOTS)]
            term = dot(source, jnp.concatenate(weights, axis=1), ((1,), (1,))).astype(BF16)
            for q in range(4):
                out[q, b] = term[32 * q : 32 * q + 32]
            return carry

        lax.fori_loop(first, first + 6, one, 0)

    def reduce_send(r, at, g, peers, blocks):
        return [
            (d, send(r.at[around(at, d), blocks], g.at[d - 1, blocks], peers[d])) for d in (2, 1, 3)
        ]

    part0, part1 = pl.ds(0, 6), pl.ds(6, 6)
    terms(pg[0], ra, 0, 0)
    a1 = reduce_send(ra, x, ga, x_peer, part0)
    terms(pgb[...], rb, 12, 0)
    b1 = reduce_send(rb, y, gb, y_peer, part0)
    terms(pg[0], ra, 0, 6)
    a2 = reduce_send(ra, x, ga, x_peer, part1)
    terms(pgb[...], rb, 12, 6)
    b2 = reduce_send(rb, y, gb, y_peer, part1)
    oth_relay()
    ring_poll(2)
    arrive(pa_part, pa.at[1])
    pa_fwd = send(pa.at[1], pa.at[3], sibling)
    arrive(pa_sib, pa.at[2])
    arrive(t_sib0, t2)
    back({2: t2})
    ring_poll(3)
    oth_finish()
    unpack(o_oth, t1)
    t_sib1 = send(t1, t3, sibling)

    def collect(r, at, g, groups, blocks):
        for sems, part in groups:
            for d, sem in sems:
                arrive(sem, g.at[d - 1, part])
        return [
            r[at, j].astype(F32) + g[0, j].astype(F32) + g[1, j].astype(F32) + g[2, j].astype(F32)
            for j in range(blocks)
        ]

    def repack(sums, out):
        for j in range(6):
            for q in range(4):
                rows = slice(8 * q, 8 * q + 8)
                both = jnp.concatenate([sums[j][rows], sums[6 + j][rows]], axis=0)
                out[q, j] = both.astype(BF16)

    whole = pl.ds(0, 6)
    repack(collect(ra, x, ga, [(a1, part0), (a2, part1)], 12), ya)
    a3 = reduce_send(ya, y, ka, y_peer, whole)
    repack(collect(rb, y, gb, [(b1, part0), (b2, part1)], 12), xb)
    b3 = reduce_send(xb, x, kb, x_peer, whole)
    arrive(pa_fwd, pa.at[3])
    arrive(t_sib1, t3)
    back({1: t1, 3: t3}, lambda: ring_poll(4))

    def total(r, at, g, sems):
        sums = collect(r, at, g, [(sems, whole)], 6)
        return [jnp.concatenate(sums[3 * q : 3 * q + 3], axis=1).astype(BF16) for q in range(2)]

    stacked = jnp.concatenate(total(ya, y, ka, a3) + total(xb, x, kb, b3), axis=0)
    order = select_rows(
        64,
        64,
        lambda r: lax.div(lax.rem(r, 16), 8) * 32
        + lax.rem(lax.div(r, 2), 2) * 16
        + lax.rem(lax.div(r, 4), 2) * 8
        + lax.div(r, 16) * 2
        + lax.rem(r, 2),
    )
    zs[...] = dot(order, stacked, ((1,), (0,))).astype(BF16).reshape(4, 16, PIECE)
    z_last = []
    for d in (3, 2, 1):
        to = around(z, d)
        z_last.append((d, send(zs.at[to], zr.at[d - 1], device(z=to))))
    ring_poll(5)

    def down(s):
        lanes = slice(s * BLK, (s + 1) * BLK)
        pick = select_rows(64, BLK, lambda r: r + dp * 64)
        mine = dot(pick, act[:, :, lanes].reshape(512, BLK), ((1,), (1,))).astype(BF16)

        def one(k, carry):
            b = col_ref[k, 2 * mp + s]
            seen = jnp.concatenate([tokens(t, b) for t in (t0, t1, t2, t3)], axis=0)
            start = pl.multiple_of(k * BLK, BLK)
            dng_ref[s, :, pl.ds(start, BLK)] = dot(mine, seen, ((1,), (0,))).astype(BF16)
            return carry

        lax.fori_loop(0, KEPT, one, 0)

    down(0)
    down(1)
    ring_poll(6)

    for d, sem in z_last:
        arrive(sem, zr.at[d - 1])
    normed_grad = (
        zs[z].astype(F32) + zr[0].astype(F32) + zr[1].astype(F32) + zr[2].astype(F32)
    )
    scaled = normed_grad * gain16[...]
    unit_rows = unit16[...]
    pack[...] = inv16[:, 0:1] * (
        scaled - token_mean(scaled) - unit_rows * token_mean(scaled * unit_rows)
    )
    for p in range(PIECES):
        gin_ref[:, p * PIECE : (p + 1) * PIECE] = pack[2 * p : 2 * p + 2, :].astype(BF16)

    def z_order(r):
        at = lax.div(r, 32)
        near = lax.rem(lax.div(at, 4) + h, 2)
        return near * 128 + lax.div(lax.rem(r, 32), 2) * 8 + lax.rem(at, 4) * 2 + lax.rem(r, 2)

    order = select_rows(256, 256, z_order)
    for core in range(2):
        both = pg[2 * core : 2 * core + 2].reshape(256, 2 * BLK)
        pg_z[core] = dot(order, both, ((1,), (0,))).astype(BF16)

    for at, sem in nm_sib:
        arrive(sem, n_sib.at[at])

    for s in range(SLOTS):
        lanes = slice(s * BLK, (s + 1) * BLK)

        def grow_up(k, carry):
            b = row_ref[dp * 4 + k, 2 * mp + s]
            picked = jnp.concatenate(
                [
                    jnp.concatenate([n[:, 2 * b], n[:, 2 * b + 1]], axis=-1).reshape(BLK, BLK)
                    for n in (n_own, n_sib)
                ],
                axis=0,
            )
            grads = pg_z[:, :, lanes].reshape(512, BLK)
            start = pl.multiple_of(k * BLK, BLK)
            upg_ref[s, pl.ds(start, BLK), :] = dot(picked, grads, ((0,), (0,))).astype(BF16)
            return carry

        lax.fori_loop(0, 4, grow_up, 0)

    for copy in started:
        copy.wait_send()


def local(
    inputs, out_grad, pre_act, norm_gain, up_weight, down_weight, row_blocks, col_blocks, counts
):
    vmem = pl.BlockSpec(memory_space=pltpu.VMEM)
    smem = pl.BlockSpec(memory_space=pltpu.SMEM)
    hbm = pl.BlockSpec(memory_space=pltpu.HBM)
    return pl.pallas_call(
        kernel,
        out_shape=(
            pltpu.VMEM((2, FEATURES), BF16),
            pltpu.VMEM((SLOTS, 1024, BLK), BF16),
            pltpu.VMEM((SLOTS, 64, 4096), BF16),
        ),
        in_specs=[hbm, hbm, hbm, hbm, hbm, hbm, smem, smem, smem],
        out_specs=(vmem, vmem, vmem),
        scratch_shapes=[
            pltpu.VMEM((2, FEATURES), BF16),
            pltpu.VMEM((2, FEATURES), BF16),
            pltpu.VMEM((1, FEATURES), F32),
            pltpu.VMEM((SLOTS, KEPT + 1, BLK, BLK), BF16),
            pltpu.VMEM((SLOTS, BLK, 4096), BF16),
            pltpu.VMEM((128, 512), BF16),
            pltpu.VMEM((4, 128, 512), BF16),
            pltpu.VMEM((16, PIECE), F32),
            pltpu.VMEM((16, PIECE), F32),
            pltpu.VMEM((16, PIECE), F32),
            pltpu.VMEM((16, 128), F32),
            pltpu.VMEM((4, 16, PIECE), BF16),
            pltpu.VMEM((4, 16, PIECE), BF16),
            pltpu.VMEM((4, 4, 16, PIECE), BF16),
        ]
        + [pltpu.VMEM((LANES, 4, 4, 16, 128), BF16)] * 2
        + [pltpu.VMEM((2 * LANES, 128, 128), BF16)] * 4
        + [pltpu.VMEM((8, 2 * LANES, 32, 128), BF16)] * 2
        + [
            pltpu.VMEM((SLOTS, 384, BLK), F32),
            pltpu.VMEM((4, 128, 512), BF16),
            pltpu.VMEM((4, 128, 512), BF16),
            pltpu.VMEM((2, 256, 512), BF16),
            pltpu.VMEM((128, 512), BF16),
        ]
        + [pltpu.VMEM((4, 12, 32, BLK), BF16)] * 2
        + [pltpu.VMEM((3, 12, 32, BLK), BF16)] * 2
        + [pltpu.VMEM((4, 6, 16, BLK), BF16)] * 2
        + [pltpu.VMEM((3, 6, 16, BLK), BF16)] * 2
        + [
            pltpu.VMEM((4, 16, PIECE), BF16),
            pltpu.VMEM((3, 16, PIECE), BF16),
            pltpu.SMEM((48,), jnp.int32),
            pltpu.SemaphoreType.DMA((7,)),
            pltpu.SemaphoreType.DMA((N_COPIES,)),
            pltpu.SemaphoreType.DMA((N_COPIES,)),
        ],
        compiler_params=pltpu.CompilerParams(
            collective_id=0, has_side_effects=True, vmem_limit_bytes=56 * 1024 * 1024
        ),
    )(
        inputs,
        out_grad,
        pre_act,
        norm_gain.reshape(1, FEATURES),
        up_weight.reshape(SLOTS, KEPT, BLK, BLK),
        down_weight,
        row_blocks.T,
        col_blocks.T,
        counts,
    )


def solution(mesh):
    placed = (
        P(("dp", "mp"), None),
        P(("dp", "mp"), None),
        P("dp", "mp"),
        P(),
        P("mp", None, None),
        P("mp", None, None),
        P(),
        P(),
        P(),
    )
    return jax.shard_map(
        local,
        mesh=mesh,
        in_specs=placed,
        out_specs=(P(("dp", "mp"), None), P("mp", "dp", None), P("mp", "dp", None)),
        check_vma=False,
    )
```

```python
import math

import jax
import jax.numpy as jnp
from jax import lax
from jax.experimental import pallas as pl
from jax.experimental.pallas import tpu as pltpu
from jax.sharding import PartitionSpec as P

EPS = 1e-06
F32 = jnp.float32
BF16 = jnp.bfloat16
PIECES = 8
PIECE = 768
BLK = 256
SLOTS = 2
KEPT = 16
FEATURES = 6144
LANES = 24
N_COPIES = 112


def dot(a, b, dims):
    return lax.dot_general(a, b, (dims, ((), ())), preferred_element_type=F32)


def select_rows(rows, columns, source_of):
    r = lax.broadcasted_iota(jnp.int32, (rows, columns), 0)
    c = lax.broadcasted_iota(jnp.int32, (rows, columns), 1)
    return (c == source_of(r)).astype(BF16)


def gelu_pair(z):
    a = math.sqrt(2.0 / math.pi)
    z2 = z * z
    t = jnp.tanh(a * z * (1.0 + 0.044715 * z2))
    half = 0.5 * (1.0 + t)
    slope = half + 0.5 * z * (1.0 - t * t) * (a * (1.0 + 3.0 * 0.044715 * z2))
    return z * half, slope


def kernel(
    x_hbm, og_hbm, pre_hbm, gain_hbm, up_hbm, dn_hbm, row_ref, col_ref, cnt_ref,
    gin_ref, upg_ref, dng_ref,
    x_ref, og_ref, gain_ref, up, dn, pre, pa,
    pack, gain16, unit16, inv16,
    raw_own, raw_oth, raw_nm,
    o_own, o_oth, t0, t1, t2, t3, n_own, n_sib,
    acc, act, pg, pg_z, pgb,
    ra, rb, ga, gb, ya, xb, ka, kb,
    zs, zr, pos,
    local_sem, send_sem, recv_sem,
):
    dp = lax.axis_index("dp")
    mp = lax.axis_index("mp")
    h, c = lax.div(dp, 2), lax.rem(dp, 2)
    z, x, y = lax.div(mp, 16), lax.rem(lax.div(mp, 4), 4), lax.rem(mp, 4)
    z8 = h * 4 + z

    def device(h=h, c=c, z=z, x=x, y=y):
        return {"dp": h * 2 + c, "mp": z * 16 + x * 4 + y}

    def around(at, by, n=4):
        return lax.rem(at + by + n, n)

    def z_device(at):
        return device(h=lax.div(at, 4), z=lax.rem(at, 4))

    x_peer = {d: device(x=around(x, d)) for d in (1, 2, 3)}
    y_peer = {d: device(y=around(y, d)) for d in (1, 2, 3)}
    z_plus, z_minus = z_device(around(z8, 1, 8)), z_device(around(z8, -1, 8))
    sibling = device(c=1 - c)
    partner = device(h=1 - h)

    started = []
    count = [0]

    def send(src, dst, target):
        k = count[0]
        count[0] += 1
        copy = pltpu.make_async_remote_copy(
            src_ref=src, dst_ref=dst, send_sem=send_sem.at[k], recv_sem=recv_sem.at[k],
            device_id=target, device_id_type=pl.DeviceIdType.MESH,
        )
        copy.start()
        started.append(copy)
        return k

    def arrive(k, dst):
        pltpu.make_async_remote_copy(
            src_ref=dst, dst_ref=dst, send_sem=send_sem.at[k], recv_sem=recv_sem.at[k],
            device_id=sibling, device_id_type=pl.DeviceIdType.MESH,
        ).wait_recv()

    def fetch(src, dst, k):
        copy = pltpu.make_async_copy(src, dst, local_sem.at[k])
        copy.start()
        return copy

    og_copy = fetch(og_hbm, og_ref, 0)
    x_copy = fetch(x_hbm, x_ref, 1)
    gain_copy = fetch(gain_hbm, gain_ref, 2)
    pre_copy = fetch(pre_hbm, pre, 3)

    barrier = pltpu.get_barrier_semaphore()
    greeted = [z_device(around(z8, k, 8)) for k in range(1, 8)]
    greeted += list(x_peer.values()) + list(y_peer.values()) + [sibling]
    for target in greeted:
        pl.semaphore_signal(
            barrier, inc=1, device_id=target, device_id_type=pl.DeviceIdType.MESH
        )

    weight_copies = [fetch(dn_hbm, dn, 4)]
    weight_copies += [fetch(up_hbm.at[s], up.at[s, pl.ds(0, KEPT)], 5 + s) for s in range(SLOTS)]

    og_copy.wait()
    for p in range(PIECES):
        pack[2 * p : 2 * p + 2, :] = og_ref[:, p * PIECE : (p + 1) * PIECE].astype(F32)
    raw_own[z] = pack[...].astype(BF16)
    x_copy.wait()
    gain_copy.wait()
    for p in range(PIECES):
        pack[2 * p : 2 * p + 2, :] = x_ref[:, p * PIECE : (p + 1) * PIECE].astype(F32)
        gain16[2 * p : 2 * p + 2, :] = jnp.broadcast_to(
            gain_ref[:, p * PIECE : (p + 1) * PIECE], (2, PIECE)
        )
    first = lax.rem(lax.broadcasted_iota(jnp.int32, (16, 1), 0), 2) == 0

    def token_mean(values):
        rows = jnp.sum(values, axis=1, keepdims=True)
        total0 = jnp.sum(jnp.where(first, rows, 0.0), axis=0, keepdims=True)
        total1 = jnp.sum(jnp.where(first, 0.0, rows), axis=0, keepdims=True)
        return jnp.where(first, total0, total1) * (1.0 / FEATURES)

    widened = pack[...]
    centred = widened - token_mean(widened)
    inv_std = lax.rsqrt(token_mean(centred * centred) + EPS)
    unit_rows = centred * inv_std
    unit16[...] = unit_rows
    inv16[...] = jnp.broadcast_to(inv_std, (16, 128))
    raw_nm[y, x] = (unit_rows * gain16[...]).astype(BF16)

    pl.semaphore_wait(barrier, len(greeted))

    own_z = [
        (d, send(raw_own.at[z], raw_own.at[z], device(z=around(z, d)))) for d in (1, 2, 3)
    ]
    cut_a, cut_b = pl.ds(0, PIECE // 2), pl.ds(PIECE // 2, PIECE // 2)
    a, b = raw_nm.at[y, x, :, cut_a], raw_nm.at[y, x, :, cut_b]
    nm_1 = [(d, send(a, a, x_peer[d]), send(b, b, y_peer[d])) for d in (1, 3, 2)]

    def place(raw, tiles, arrivals):
        for d, sem in arrivals:
            arrive(sem, raw.at[around(z, -d)])
        order = select_rows(
            64,
            64,
            lambda r: lax.div(lax.rem(r, 8), 2) * 16
            + lax.div(lax.rem(r, 16), 8) * 8
            + lax.div(r, 16) * 2
            + lax.rem(r, 2),
        )
        out = dot(order, raw[...].reshape(64, PIECE), ((1,), (0,))).astype(BF16)
        for p in range(4):
            for q in range(6):
                tiles[p * 6 + q, x, y] = out[16 * p : 16 * p + 16, 128 * q : 128 * q + 128]

    lane_a, lane_b = pl.ds(0, 12), pl.ds(12, 12)

    def narrow_send(o):
        a, b = o.at[lane_a, x, y], o.at[lane_b, x, y]
        return [(d, send(a, a, x_peer[d]), send(b, b, y_peer[d])) for d in (1, 3, 2)]

    def column_send(o, at_x, at_y):
        a, b = o.at[lane_a, at_x, y], o.at[lane_b, x, at_y]
        return [(d, send(a, a, y_peer[d]), send(b, b, x_peer[d])) for d in (1, 3, 2)]

    def narrow_wait(o, sem):
        d, sem_a, sem_b = sem
        arrive(sem_a, o.at[lane_a, around(x, -d), y])
        arrive(sem_b, o.at[lane_b, x, around(y, -d)])

    place(raw_own, o_own, own_z)
    own_n = narrow_send(o_own)
    own_w = [(0, column_send(o_own, x, y))]
    oth_z = [
        (d, send(raw_own.at[z], raw_oth.at[z], device(h=1 - h, z=around(z, d)))) for d in range(4)
    ]
    for d, sem_a, sem_b in nm_1:
        arrive(sem_a, raw_nm.at[y, around(x, -d), :, cut_a])
        arrive(sem_b, raw_nm.at[around(y, -d), x, :, cut_b])
    a, b = raw_nm.at[y, :, :, cut_a], raw_nm.at[:, x, :, cut_b]
    nm_2 = [(d, send(a, a, y_peer[d]), send(b, b, x_peer[d])) for d in (1, 3, 2)]

    pre_copy.wait()
    order = select_rows(
        128, 128, lambda r: lax.div(lax.rem(r, 8), 2) * 32 + lax.div(r, 8) * 2 + lax.rem(r, 2)
    )
    pa[0] = dot(order, pre[...], ((1,), (0,))).astype(BF16)
    pa_part = send(pa.at[0], pa.at[1], partner)
    pa_sib = send(pa.at[0], pa.at[2], sibling)

    for s in range(SLOTS):
        up[s, KEPT] = jnp.zeros((BLK, BLK), BF16)

    def locate(b, carry):
        for s in range(SLOTS):
            found = jnp.int32(KEPT)
            for k in range(KEPT):
                found = jnp.where(row_ref[k, 2 * mp + s] == b, k, found)
            pos[s * 24 + b] = found
        return carry

    lax.fori_loop(0, 24, locate, 0)
    for sem in own_n:
        narrow_wait(o_own, sem)
        own_w.append((sem[0], column_send(o_own, around(x, -sem[0]), around(y, -sem[0]))))

    for d, sem_a, sem_b in nm_2:
        arrive(sem_a, raw_nm.at[around(y, -d), :, :, cut_a])
        arrive(sem_b, raw_nm.at[:, around(x, -d), :, cut_b])
    order = select_rows(
        256,
        256,
        lambda r: lax.div(lax.rem(r, 8), 2) * 64
        + lax.div(lax.rem(r, 32), 8) * 16
        + lax.div(r, 32) * 2
        + lax.rem(r, 2),
    )
    out = dot(order, raw_nm[...].reshape(256, PIECE), ((1,), (0,))).astype(BF16)
    for p in range(PIECES):
        for q in range(6):
            n_own[z8, p * 6 + q] = out[32 * p : 32 * p + 32, 128 * q : 128 * q + 128]

    steps = [(0, 0), (0, 1), (1, 0), (1, 1), (2, 0), (2, 1), (3, 0)]
    halves = (pl.ds(0, 24), pl.ds(24, 24))
    nm_sems = {}

    def ring_send(n):
        far, half = steps[n]
        plus = n_own.at[around(z8, -far, 8), halves[half]]
        minus = n_own.at[around(z8, far, 8), halves[1 - half]]
        nm_sems[n] = (send(plus, plus, z_plus), send(minus, minus, z_minus))

    nm_sib = []

    def to_sibling(at):
        nm_sib.append((at, send(n_own.at[at], n_sib.at[at], sibling)))

    def ring_poll(n):
        far, half = steps[n]
        arrive(nm_sems[n][0], n_own.at[around(z8, -far - 1, 8), halves[half]])
        arrive(nm_sems[n][1], n_own.at[around(z8, far + 1, 8), halves[1 - half]])
        if n + 2 < len(steps):
            ring_send(n + 2)
        if half == 1:
            to_sibling(around(z8, far + 1, 8))
            to_sibling(around(z8, -far - 1, 8))
        if n == 6:
            to_sibling(around(z8, 4, 8))

    ring_send(0)
    ring_send(1)
    to_sibling(z8)

    place(raw_oth, o_oth, oth_z)
    oth_n = narrow_send(o_oth)
    for copy in weight_copies:
        copy.wait()
    for far, sems in own_w:
        for d, sem_a, sem_b in sems:
            arrive(sem_a, o_own.at[lane_a, around(x, -far), around(y, -d)])
            arrive(sem_b, o_own.at[lane_b, around(x, -d), around(y, -far)])
    for sem in oth_n:
        narrow_wait(o_oth, sem)

    def wide_send(o, lanes_a, lanes_b, from_x, from_y, d):
        a, b = o.at[lanes_a, :, from_y], o.at[lanes_b, from_x]
        return send(a, a, y_peer[d]), send(b, b, x_peer[d])

    def wide_wait(o, lanes_a, lanes_b, sems, d):
        arrive(sems[0], o.at[lanes_a, :, around(y, -d)])
        arrive(sems[1], o.at[lanes_b, around(x, -d)])

    quarter = [pl.ds(6 * k, 6) for k in range(4)]
    oth_w = {d: wide_send(o_oth, lane_a, lane_b, x, y, d) for d in (1, 3)}

    def oth_relay():
        for d, qa, qb in ((1, quarter[0], quarter[2]), (3, quarter[1], quarter[3])):
            wide_wait(o_oth, lane_a, lane_b, oth_w[d], d)
            oth_w[d + 10] = wide_send(o_oth, qa, qb, around(x, -d), around(y, -d), d)

    def oth_finish():
        wide_wait(o_oth, quarter[0], quarter[2], oth_w[11], 2)
        wide_wait(o_oth, quarter[1], quarter[3], oth_w[13], 2)

    ring_poll(0)

    def unpack(o, t):
        def one(k, carry):
            rows = o[k].astype(F32).reshape(16, 2, 8, 128)
            t[k] = rows[:, 0].reshape(128, 128).astype(BF16)
            t[LANES + k] = rows[:, 1].reshape(128, 128).astype(BF16)
            return carry

        lax.fori_loop(0, LANES, one, 0, unroll=4)

    unpack(o_own, t0)
    t_sib0 = send(t0, t2, sibling)

    live = [s < cnt_ref[mp] for s in range(SLOTS)]

    def tokens(t, b):
        return jnp.concatenate([t[2 * b], t[2 * b + 1]], axis=-1)

    def back(groups, between=lambda: None):
        rows = 128 * len(groups)
        for s in range(SLOTS):
            acc[s, 0:rows] = jnp.zeros((rows, BLK), F32)

            def grow(k, carry):
                parts = []
                for j in range(4):
                    b = col_ref[4 * k + j, 2 * mp + s]
                    parts.append(jnp.concatenate([tokens(t, b) for t in groups.values()], axis=0))
                start = pl.multiple_of(k * 1024, 1024)
                term = dot(
                    jnp.concatenate(parts, axis=1), dn[s, :, pl.ds(start, 1024)], ((1,), (1,))
                )

                acc[s, 0:rows] += term
                return carry

            lax.fori_loop(0, KEPT // 4, grow, 0, unroll=True)
            if s == 0:
                between()

        def derive(j, carry):
            at = pl.ds(pl.multiple_of(j * 16, 16), 16)
            for n, g in enumerate(groups):
                for s in range(SLOTS):
                    lanes = slice(s * BLK, (s + 1) * BLK)
                    value, slope = gelu_pair(pa[g, at, lanes].astype(F32))
                    grad = acc[s, pl.ds(pl.multiple_of(n * 128 + j * 16, 16), 16), :] * slope
                    pg[g, at, lanes] = jnp.where(live[s], grad, 0.0).astype(BF16)
                    act[g, at, lanes] = jnp.where(live[s], value, 0.0).astype(BF16)
            return carry

        lax.fori_loop(0, 8, derive, 0, unroll=4)

    back({0: t0}, lambda: ring_poll(1))

    order = select_rows(
        128, 128, lambda r: lax.div(lax.rem(r, 32), 8) * 32 + lax.div(r, 32) * 8 + lax.rem(r, 8)
    )
    pgb[...] = dot(order, pg[0], ((1,), (0,))).astype(BF16)

    def terms(source, out, base, first):
        def one(b, carry):
            weights = [up[s, pos[s * 24 + base + b]] for s in range(SLOTS)]
            term = dot(source, jnp.concatenate(weights, axis=1), ((1,), (1,))).astype(BF16)
            for q in range(4):
                out[q, b] = term[32 * q : 32 * q + 32]
            return carry

        lax.fori_loop(first, first + 6, one, 0, unroll=True)

    def reduce_send(r, at, g, peers, blocks):
        return [
            (d, send(r.at[around(at, d), blocks], g.at[d - 1, blocks], peers[d])) for d in (2, 1, 3)
        ]

    part0, part1 = pl.ds(0, 6), pl.ds(6, 6)
    terms(pg[0], ra, 0, 0)
    a1 = reduce_send(ra, x, ga, x_peer, part0)
    terms(pgb[...], rb, 12, 0)
    b1 = reduce_send(rb, y, gb, y_peer, part0)
    terms(pg[0], ra, 0, 6)
    a2 = reduce_send(ra, x, ga, x_peer, part1)
    terms(pgb[...], rb, 12, 6)
    b2 = reduce_send(rb, y, gb, y_peer, part1)
    oth_relay()
    ring_poll(2)
    arrive(pa_part, pa.at[1])
    pa_fwd = send(pa.at[1], pa.at[3], sibling)
    arrive(pa_sib, pa.at[2])
    arrive(t_sib0, t2)
    back({2: t2})
    ring_poll(3)
    oth_finish()
    unpack(o_oth, t1)
    t_sib1 = send(t1, t3, sibling)

    def collect(r, at, g, groups, blocks):
        for sems, part in groups:
            for d, sem in sems:
                arrive(sem, g.at[d - 1, part])
        return [
            r[at, j].astype(F32) + g[0, j].astype(F32) + g[1, j].astype(F32) + g[2, j].astype(F32)
            for j in range(blocks)
        ]

    def repack(sums, out):
        for j in range(6):
            for q in range(4):
                rows = slice(8 * q, 8 * q + 8)
                both = jnp.concatenate([sums[j][rows], sums[6 + j][rows]], axis=0)
                out[q, j] = both.astype(BF16)

    whole = pl.ds(0, 6)
    repack(collect(ra, x, ga, [(a1, part0), (a2, part1)], 12), ya)
    a3 = reduce_send(ya, y, ka, y_peer, whole)
    repack(collect(rb, y, gb, [(b1, part0), (b2, part1)], 12), xb)
    b3 = reduce_send(xb, x, kb, x_peer, whole)
    arrive(pa_fwd, pa.at[3])
    arrive(t_sib1, t3)
    back({1: t1, 3: t3}, lambda: ring_poll(4))

    def total(r, at, g, sems):
        sums = collect(r, at, g, [(sems, whole)], 6)
        return [jnp.concatenate(sums[3 * q : 3 * q + 3], axis=1).astype(BF16) for q in range(2)]

    stacked = jnp.concatenate(total(ya, y, ka, a3) + total(xb, x, kb, b3), axis=0)
    order = select_rows(
        64,
        64,
        lambda r: lax.div(lax.rem(r, 16), 8) * 32
        + lax.rem(lax.div(r, 2), 2) * 16
        + lax.rem(lax.div(r, 4), 2) * 8
        + lax.div(r, 16) * 2
        + lax.rem(r, 2),
    )
    zs[...] = dot(order, stacked, ((1,), (0,))).astype(BF16).reshape(4, 16, PIECE)
    z_last = []
    for d in (3, 2, 1):
        to = around(z, d)
        z_last.append((d, send(zs.at[to], zr.at[d - 1], device(z=to))))
    ring_poll(5)

    def down(s):
        lanes = slice(s * BLK, (s + 1) * BLK)
        pick = select_rows(64, BLK, lambda r: r + dp * 64)
        mine = dot(pick, act[:, :, lanes].reshape(512, BLK), ((1,), (1,))).astype(BF16)

        def one(k, carry):
            b = col_ref[k, 2 * mp + s]
            seen = jnp.concatenate([tokens(t, b) for t in (t0, t1, t2, t3)], axis=0)
            start = pl.multiple_of(k * BLK, BLK)
            dng_ref[s, :, pl.ds(start, BLK)] = dot(mine, seen, ((1,), (0,))).astype(BF16)
            return carry

        lax.fori_loop(0, KEPT, one, 0, unroll=8)

    down(0)
    down(1)
    ring_poll(6)

    for d, sem in z_last:
        arrive(sem, zr.at[d - 1])
    normed_grad = (
        zs[z].astype(F32) + zr[0].astype(F32) + zr[1].astype(F32) + zr[2].astype(F32)
    )
    scaled = normed_grad * gain16[...]
    unit_rows = unit16[...]
    pack[...] = inv16[:, 0:1] * (
        scaled - token_mean(scaled) - unit_rows * token_mean(scaled * unit_rows)
    )
    for p in range(PIECES):
        gin_ref[:, p * PIECE : (p + 1) * PIECE] = pack[2 * p : 2 * p + 2, :].astype(BF16)

    def z_order(r):
        at = lax.div(r, 32)
        near = lax.rem(lax.div(at, 4) + h, 2)
        return near * 128 + lax.div(lax.rem(r, 32), 2) * 8 + lax.rem(at, 4) * 2 + lax.rem(r, 2)

    order = select_rows(256, 256, z_order)
    for core in range(2):
        both = pg[2 * core : 2 * core + 2].reshape(256, 2 * BLK)
        pg_z[core] = dot(order, both, ((1,), (0,))).astype(BF16)

    for at, sem in nm_sib:
        arrive(sem, n_sib.at[at])

    for s in range(SLOTS):
        lanes = slice(s * BLK, (s + 1) * BLK)

        def grow_up(k, carry):
            b = row_ref[dp * 4 + k, 2 * mp + s]
            picked = jnp.concatenate(
                [
                    jnp.concatenate([n[:, 2 * b], n[:, 2 * b + 1]], axis=-1).reshape(BLK, BLK)
                    for n in (n_own, n_sib)
                ],
                axis=0,
            )
            grads = pg_z[:, :, lanes].reshape(512, BLK)
            start = pl.multiple_of(k * BLK, BLK)
            upg_ref[s, pl.ds(start, BLK), :] = dot(picked, grads, ((0,), (0,))).astype(BF16)
            return carry

        lax.fori_loop(0, 4, grow_up, 0, unroll=True)

    for copy in started:
        copy.wait_send()


def local(
    inputs, out_grad, pre_act, norm_gain, up_weight, down_weight, row_blocks, col_blocks, counts
):
    vmem = pl.BlockSpec(memory_space=pltpu.VMEM)
    smem = pl.BlockSpec(memory_space=pltpu.SMEM)
    hbm = pl.BlockSpec(memory_space=pltpu.HBM)
    return pl.pallas_call(
        kernel,
        out_shape=(
            pltpu.VMEM((2, FEATURES), BF16),
            pltpu.VMEM((SLOTS, 1024, BLK), BF16),
            pltpu.VMEM((SLOTS, 64, 4096), BF16),
        ),
        in_specs=[hbm, hbm, hbm, hbm, hbm, hbm, smem, smem, smem],
        out_specs=(vmem, vmem, vmem),
        scratch_shapes=[
            pltpu.VMEM((2, FEATURES), BF16),
            pltpu.VMEM((2, FEATURES), BF16),
            pltpu.VMEM((1, FEATURES), F32),
            pltpu.VMEM((SLOTS, KEPT + 1, BLK, BLK), BF16),
            pltpu.VMEM((SLOTS, BLK, 4096), BF16),
            pltpu.VMEM((128, 512), BF16),
            pltpu.VMEM((4, 128, 512), BF16),
            pltpu.VMEM((16, PIECE), F32),
            pltpu.VMEM((16, PIECE), F32),
            pltpu.VMEM((16, PIECE), F32),
            pltpu.VMEM((16, 128), F32),
            pltpu.VMEM((4, 16, PIECE), BF16),
            pltpu.VMEM((4, 16, PIECE), BF16),
            pltpu.VMEM((4, 4, 16, PIECE), BF16),
        ]
        + [pltpu.VMEM((LANES, 4, 4, 16, 128), BF16)] * 2
        + [pltpu.VMEM((2 * LANES, 128, 128), BF16)] * 4
        + [pltpu.VMEM((8, 2 * LANES, 32, 128), BF16)] * 2
        + [
            pltpu.VMEM((SLOTS, 384, BLK), F32),
            pltpu.VMEM((4, 128, 512), BF16),
            pltpu.VMEM((4, 128, 512), BF16),
            pltpu.VMEM((2, 256, 512), BF16),
            pltpu.VMEM((128, 512), BF16),
        ]
        + [pltpu.VMEM((4, 12, 32, BLK), BF16)] * 2
        + [pltpu.VMEM((3, 12, 32, BLK), BF16)] * 2
        + [pltpu.VMEM((4, 6, 16, BLK), BF16)] * 2
        + [pltpu.VMEM((3, 6, 16, BLK), BF16)] * 2
        + [
            pltpu.VMEM((4, 16, PIECE), BF16),
            pltpu.VMEM((3, 16, PIECE), BF16),
            pltpu.SMEM((48,), jnp.int32),
            pltpu.SemaphoreType.DMA((7,)),
            pltpu.SemaphoreType.DMA((N_COPIES,)),
            pltpu.SemaphoreType.DMA((N_COPIES,)),
        ],
        compiler_params=pltpu.CompilerParams(
            collective_id=0, has_side_effects=True, vmem_limit_bytes=56 * 1024 * 1024
        ),
    )(
        inputs,
        out_grad,
        pre_act,
        norm_gain.reshape(1, FEATURES),
        up_weight.reshape(SLOTS, KEPT, BLK, BLK),
        down_weight,
        row_blocks.T,
        col_blocks.T,
        counts,
    )


def solution(mesh):
    placed = (
        P(("dp", "mp"), None),
        P(("dp", "mp"), None),
        P("dp", "mp"),
        P(),
        P("mp", None, None),
        P("mp", None, None),
        P(),
        P(),
        P(),
    )
    return jax.shard_map(
        local,
        mesh=mesh,
        in_specs=placed,
        out_specs=(P(("dp", "mp"), None), P("mp", "dp", None), P("mp", "dp", None)),
        check_vma=False,
    )
```

```python
import math

import jax
import jax.numpy as jnp
from jax import lax
from jax.experimental import pallas as pl
from jax.experimental.pallas import tpu as pltpu
from jax.sharding import PartitionSpec as P

EPS = 1e-06
F32 = jnp.float32
BF16 = jnp.bfloat16
PIECES = 8
PIECE = 768
BLK = 256
SLOTS = 2
KEPT = 16
FEATURES = 6144
LANES = 24
N_COPIES = 112


def dot(a, b, dims):
    return lax.dot_general(a, b, (dims, ((), ())), preferred_element_type=F32)


def select_rows(rows, columns, source_of):
    r = lax.broadcasted_iota(jnp.int32, (rows, columns), 0)
    c = lax.broadcasted_iota(jnp.int32, (rows, columns), 1)
    return (c == source_of(r)).astype(BF16)


def gelu_pair(z):
    a = math.sqrt(2.0 / math.pi)
    z2 = z * z
    t = jnp.tanh(a * z * (1.0 + 0.044715 * z2))
    half = 0.5 * (1.0 + t)
    slope = half + 0.5 * z * (1.0 - t * t) * (a * (1.0 + 3.0 * 0.044715 * z2))
    return z * half, slope


def kernel(
    x_hbm, og_hbm, pre_hbm, gain_hbm, up_hbm, dn_hbm, row_ref, col_ref, cnt_ref,
    gin_ref, upg_ref, dng_ref,
    x_ref, og_ref, gain_ref, up, dn, pre, pa,
    pack, gain16, unit16, inv16,
    raw_own, raw_oth, raw_nm,
    o_own, o_oth, t0, t1, t2, t3, n_own, n_sib,
    acc, act, pg, pg_z, pgb, up_own,
    ra, rb, ga, gb, ya, xb, ka, kb,
    zs, zr, pos,
    local_sem, send_sem, recv_sem,
):
    dp = lax.axis_index("dp")
    mp = lax.axis_index("mp")
    h, c = lax.div(dp, 2), lax.rem(dp, 2)
    z, x, y = lax.div(mp, 16), lax.rem(lax.div(mp, 4), 4), lax.rem(mp, 4)
    z8 = h * 4 + z

    def device(h=h, c=c, z=z, x=x, y=y):
        return {"dp": h * 2 + c, "mp": z * 16 + x * 4 + y}

    def around(at, by, n=4):
        return lax.rem(at + by + n, n)

    def z_device(at):
        return device(h=lax.div(at, 4), z=lax.rem(at, 4))

    x_peer = {d: device(x=around(x, d)) for d in (1, 2, 3)}
    y_peer = {d: device(y=around(y, d)) for d in (1, 2, 3)}
    z_plus, z_minus = z_device(around(z8, 1, 8)), z_device(around(z8, -1, 8))
    sibling = device(c=1 - c)
    partner = device(h=1 - h)

    started = []
    count = [0]

    def send(src, dst, target):
        k = count[0]
        count[0] += 1
        copy = pltpu.make_async_remote_copy(
            src_ref=src, dst_ref=dst, send_sem=send_sem.at[k], recv_sem=recv_sem.at[k],
            device_id=target, device_id_type=pl.DeviceIdType.MESH,
        )
        copy.start()
        started.append(copy)
        return k

    def arrive(k, dst):
        pltpu.make_async_remote_copy(
            src_ref=dst, dst_ref=dst, send_sem=send_sem.at[k], recv_sem=recv_sem.at[k],
            device_id=sibling, device_id_type=pl.DeviceIdType.MESH,
        ).wait_recv()

    def fetch(src, dst, k):
        copy = pltpu.make_async_copy(src, dst, local_sem.at[k])
        copy.start()
        return copy

    og_copy = fetch(og_hbm, og_ref, 0)
    x_copy = fetch(x_hbm, x_ref, 1)
    gain_copy = fetch(gain_hbm, gain_ref, 2)
    pre_copy = fetch(pre_hbm, pre, 3)

    barrier = pltpu.get_barrier_semaphore()
    greeted = [z_device(around(z8, k, 8)) for k in range(1, 8)]
    greeted += list(x_peer.values()) + list(y_peer.values()) + [sibling]
    for target in greeted:
        pl.semaphore_signal(
            barrier, inc=1, device_id=target, device_id_type=pl.DeviceIdType.MESH
        )

    weight_copies = [fetch(dn_hbm, dn, 4)]
    weight_copies += [fetch(up_hbm.at[s], up.at[s, pl.ds(0, KEPT)], 5 + s) for s in range(SLOTS)]

    og_copy.wait()
    for p in range(PIECES):
        pack[2 * p : 2 * p + 2, :] = og_ref[:, p * PIECE : (p + 1) * PIECE].astype(F32)
    raw_own[z] = pack[...].astype(BF16)
    x_copy.wait()
    gain_copy.wait()
    for p in range(PIECES):
        pack[2 * p : 2 * p + 2, :] = x_ref[:, p * PIECE : (p + 1) * PIECE].astype(F32)
        gain16[2 * p : 2 * p + 2, :] = jnp.broadcast_to(
            gain_ref[:, p * PIECE : (p + 1) * PIECE], (2, PIECE)
        )
    first = lax.rem(lax.broadcasted_iota(jnp.int32, (16, 1), 0), 2) == 0

    def token_mean(values):
        rows = jnp.sum(values, axis=1, keepdims=True)
        total0 = jnp.sum(jnp.where(first, rows, 0.0), axis=0, keepdims=True)
        total1 = jnp.sum(jnp.where(first, 0.0, rows), axis=0, keepdims=True)
        return jnp.where(first, total0, total1) * (1.0 / FEATURES)

    widened = pack[...]
    centred = widened - token_mean(widened)
    inv_std = lax.rsqrt(token_mean(centred * centred) + EPS)
    unit_rows = centred * inv_std
    unit16[...] = unit_rows
    inv16[...] = jnp.broadcast_to(inv_std, (16, 128))
    raw_nm[y, x] = (unit_rows * gain16[...]).astype(BF16)

    pl.semaphore_wait(barrier, len(greeted))

    own_z = [
        (d, send(raw_own.at[z], raw_own.at[z], device(z=around(z, d)))) for d in (1, 2, 3)
    ]
    cut_a, cut_b = pl.ds(0, PIECE // 2), pl.ds(PIECE // 2, PIECE // 2)
    a, b = raw_nm.at[y, x, :, cut_a], raw_nm.at[y, x, :, cut_b]
    nm_1 = [(d, send(a, a, x_peer[d]), send(b, b, y_peer[d])) for d in (1, 3, 2)]

    def place(raw, tiles, arrivals):
        for d, sem in arrivals:
            arrive(sem, raw.at[around(z, -d)])
        order = select_rows(
            64,
            64,
            lambda r: lax.div(lax.rem(r, 8), 2) * 16
            + lax.div(lax.rem(r, 16), 8) * 8
            + lax.div(r, 16) * 2
            + lax.rem(r, 2),
        )
        out = dot(order, raw[...].reshape(64, PIECE), ((1,), (0,))).astype(BF16)
        for p in range(4):
            for q in range(6):
                tiles[p * 6 + q, x, y] = out[16 * p : 16 * p + 16, 128 * q : 128 * q + 128]

    lane_a, lane_b = pl.ds(0, 12), pl.ds(12, 12)

    def narrow_send(o):
        a, b = o.at[lane_a, x, y], o.at[lane_b, x, y]
        return [(d, send(a, a, x_peer[d]), send(b, b, y_peer[d])) for d in (1, 3, 2)]

    def column_send(o, at_x, at_y):
        a, b = o.at[lane_a, at_x, y], o.at[lane_b, x, at_y]
        return [(d, send(a, a, y_peer[d]), send(b, b, x_peer[d])) for d in (1, 3, 2)]

    def narrow_wait(o, sem):
        d, sem_a, sem_b = sem
        arrive(sem_a, o.at[lane_a, around(x, -d), y])
        arrive(sem_b, o.at[lane_b, x, around(y, -d)])

    place(raw_own, o_own, own_z)
    own_n = narrow_send(o_own)
    own_w = [(0, column_send(o_own, x, y))]
    oth_z = [
        (d, send(raw_own.at[z], raw_oth.at[z], device(h=1 - h, z=around(z, d)))) for d in range(4)
    ]
    for d, sem_a, sem_b in nm_1:
        arrive(sem_a, raw_nm.at[y, around(x, -d), :, cut_a])
        arrive(sem_b, raw_nm.at[around(y, -d), x, :, cut_b])
    a, b = raw_nm.at[y, :, :, cut_a], raw_nm.at[:, x, :, cut_b]
    nm_2 = [(d, send(a, a, y_peer[d]), send(b, b, x_peer[d])) for d in (1, 3, 2)]

    pre_copy.wait()
    order = select_rows(
        128, 128, lambda r: lax.div(lax.rem(r, 8), 2) * 32 + lax.div(r, 8) * 2 + lax.rem(r, 2)
    )
    pa[0] = dot(order, pre[...], ((1,), (0,))).astype(BF16)
    pa_part = send(pa.at[0], pa.at[1], partner)
    pa_sib = send(pa.at[0], pa.at[2], sibling)

    for s in range(SLOTS):
        up[s, KEPT] = jnp.zeros((BLK, BLK), BF16)

    def locate(b, carry):
        for s in range(SLOTS):
            found = jnp.int32(KEPT)
            for k in range(KEPT):
                found = jnp.where(row_ref[k, 2 * mp + s] == b, k, found)
            pos[s * 24 + b] = found
        return carry

    lax.fori_loop(0, 24, locate, 0)
    for sem in own_n:
        narrow_wait(o_own, sem)
        own_w.append((sem[0], column_send(o_own, around(x, -sem[0]), around(y, -sem[0]))))

    for d, sem_a, sem_b in nm_2:
        arrive(sem_a, raw_nm.at[around(y, -d), :, :, cut_a])
        arrive(sem_b, raw_nm.at[:, around(x, -d), :, cut_b])
    order = select_rows(
        256,
        256,
        lambda r: lax.div(lax.rem(r, 8), 2) * 64
        + lax.div(lax.rem(r, 32), 8) * 16
        + lax.div(r, 32) * 2
        + lax.rem(r, 2),
    )
    out = dot(order, raw_nm[...].reshape(256, PIECE), ((1,), (0,))).astype(BF16)
    for p in range(PIECES):
        for q in range(6):
            n_own[z8, p * 6 + q] = out[32 * p : 32 * p + 32, 128 * q : 128 * q + 128]

    steps = [(0, 0), (0, 1), (1, 0), (1, 1), (2, 0), (2, 1), (3, 0)]
    halves = (pl.ds(0, 24), pl.ds(24, 24))
    nm_sems = {}

    def ring_send(n):
        far, half = steps[n]
        plus = n_own.at[around(z8, -far, 8), halves[half]]
        minus = n_own.at[around(z8, far, 8), halves[1 - half]]
        nm_sems[n] = (send(plus, plus, z_plus), send(minus, minus, z_minus))

    nm_sib = []

    def to_sibling(at):
        nm_sib.append((at, send(n_own.at[at], n_sib.at[at], sibling)))

    def ring_poll(n):
        far, half = steps[n]
        arrive(nm_sems[n][0], n_own.at[around(z8, -far - 1, 8), halves[half]])
        arrive(nm_sems[n][1], n_own.at[around(z8, far + 1, 8), halves[1 - half]])
        if n + 2 < len(steps):
            ring_send(n + 2)
        if half == 1:
            to_sibling(around(z8, far + 1, 8))
            to_sibling(around(z8, -far - 1, 8))
        if n == 6:
            to_sibling(around(z8, 4, 8))

    ring_send(0)
    ring_send(1)
    to_sibling(z8)

    place(raw_oth, o_oth, oth_z)
    oth_n = narrow_send(o_oth)
    for copy in weight_copies:
        copy.wait()
    for far, sems in own_w:
        for d, sem_a, sem_b in sems:
            arrive(sem_a, o_own.at[lane_a, around(x, -far), around(y, -d)])
            arrive(sem_b, o_own.at[lane_b, around(x, -d), around(y, -far)])
    for sem in oth_n:
        narrow_wait(o_oth, sem)

    def wide_send(o, lanes_a, lanes_b, from_x, from_y, d):
        a, b = o.at[lanes_a, :, from_y], o.at[lanes_b, from_x]
        return send(a, a, y_peer[d]), send(b, b, x_peer[d])

    def wide_wait(o, lanes_a, lanes_b, sems, d):
        arrive(sems[0], o.at[lanes_a, :, around(y, -d)])
        arrive(sems[1], o.at[lanes_b, around(x, -d)])

    quarter = [pl.ds(6 * k, 6) for k in range(4)]
    oth_w = {d: wide_send(o_oth, lane_a, lane_b, x, y, d) for d in (1, 3)}

    def oth_relay():
        for d, qa, qb in ((1, quarter[0], quarter[2]), (3, quarter[1], quarter[3])):
            wide_wait(o_oth, lane_a, lane_b, oth_w[d], d)
            oth_w[d + 10] = wide_send(o_oth, qa, qb, around(x, -d), around(y, -d), d)

    def oth_finish():
        wide_wait(o_oth, quarter[0], quarter[2], oth_w[11], 2)
        wide_wait(o_oth, quarter[1], quarter[3], oth_w[13], 2)

    ring_poll(0)

    def unpack(o, t):
        def one(k, carry):
            rows = o[k].astype(F32).reshape(16, 2, 8, 128)
            t[k] = rows[:, 0].reshape(128, 128).astype(BF16)
            t[LANES + k] = rows[:, 1].reshape(128, 128).astype(BF16)
            return carry

        lax.fori_loop(0, LANES, one, 0, unroll=4)

    unpack(o_own, t0)
    t_sib0 = send(t0, t2, sibling)

    live = [s < cnt_ref[mp] for s in range(SLOTS)]

    def tokens(t, b):
        return jnp.concatenate([t[2 * b], t[2 * b + 1]], axis=-1)

    def back(groups, between=lambda: None):
        rows = 128 * len(groups)
        for s in range(SLOTS):
            acc[s, 0:rows] = jnp.zeros((rows, BLK), F32)

            def grow(k, carry):
                parts = []
                for j in range(4):
                    b = col_ref[4 * k + j, 2 * mp + s]
                    parts.append(jnp.concatenate([tokens(t, b) for t in groups.values()], axis=0))
                start = pl.multiple_of(k * 1024, 1024)
                term = dot(
                    jnp.concatenate(parts, axis=1), dn[s, :, pl.ds(start, 1024)], ((1,), (1,))
                )

                acc[s, 0:rows] += term
                return carry

            lax.fori_loop(0, KEPT // 4, grow, 0, unroll=True)
            if s == 0:
                between()

        def derive(j, carry):
            at = pl.ds(pl.multiple_of(j * 16, 16), 16)
            for n, g in enumerate(groups):
                for s in range(SLOTS):
                    lanes = slice(s * BLK, (s + 1) * BLK)
                    value, slope = gelu_pair(pa[g, at, lanes].astype(F32))
                    grad = acc[s, pl.ds(pl.multiple_of(n * 128 + j * 16, 16), 16), :] * slope
                    pg[g, at, lanes] = jnp.where(live[s], grad, 0.0).astype(BF16)
                    act[g, at, lanes] = jnp.where(live[s], value, 0.0).astype(BF16)
            return carry

        lax.fori_loop(0, 8, derive, 0, unroll=4)

    back({0: t0}, lambda: ring_poll(1))

    order = select_rows(
        128, 128, lambda r: lax.div(lax.rem(r, 32), 8) * 32 + lax.div(r, 32) * 8 + lax.rem(r, 8)
    )
    pgb[...] = dot(order, pg[0], ((1,), (0,))).astype(BF16)

    def terms(source, out, base, first):
        def one(b, carry):
            weights = [up[s, pos[s * 24 + base + b]] for s in range(SLOTS)]
            term = dot(source, jnp.concatenate(weights, axis=1), ((1,), (1,))).astype(BF16)
            for q in range(4):
                out[q, b] = term[32 * q : 32 * q + 32]
            return carry

        lax.fori_loop(first, first + 6, one, 0, unroll=True)

    def reduce_send(r, at, g, peers, blocks):
        return [
            (d, send(r.at[around(at, d), blocks], g.at[d - 1, blocks], peers[d])) for d in (2, 1, 3)
        ]

    part0, part1 = pl.ds(0, 6), pl.ds(6, 6)
    terms(pg[0], ra, 0, 0)
    a1 = reduce_send(ra, x, ga, x_peer, part0)
    terms(pgb[...], rb, 12, 0)
    b1 = reduce_send(rb, y, gb, y_peer, part0)
    terms(pg[0], ra, 0, 6)
    a2 = reduce_send(ra, x, ga, x_peer, part1)
    terms(pgb[...], rb, 12, 6)
    b2 = reduce_send(rb, y, gb, y_peer, part1)
    oth_relay()
    ring_poll(2)
    arrive(pa_part, pa.at[1])
    pa_fwd = send(pa.at[1], pa.at[3], sibling)
    arrive(pa_sib, pa.at[2])
    arrive(t_sib0, t2)
    back({2: t2})
    ring_poll(3)
    oth_finish()
    unpack(o_oth, t1)
    t_sib1 = send(t1, t3, sibling)

    def collect(r, at, g, groups, blocks):
        for sems, part in groups:
            for d, sem in sems:
                arrive(sem, g.at[d - 1, part])
        return [
            r[at, j].astype(F32) + g[0, j].astype(F32) + g[1, j].astype(F32) + g[2, j].astype(F32)
            for j in range(blocks)
        ]

    def repack(sums, out):
        for j in range(6):
            for q in range(4):
                rows = slice(8 * q, 8 * q + 8)
                both = jnp.concatenate([sums[j][rows], sums[6 + j][rows]], axis=0)
                out[q, j] = both.astype(BF16)

    whole = pl.ds(0, 6)
    repack(collect(ra, x, ga, [(a1, part0), (a2, part1)], 12), ya)
    a3 = reduce_send(ya, y, ka, y_peer, whole)
    repack(collect(rb, y, gb, [(b1, part0), (b2, part1)], 12), xb)
    b3 = reduce_send(xb, x, kb, x_peer, whole)
    arrive(pa_fwd, pa.at[3])
    arrive(t_sib1, t3)
    back({1: t1, 3: t3}, lambda: ring_poll(4))

    def total(r, at, g, sems):
        sums = collect(r, at, g, [(sems, whole)], 6)
        return [jnp.concatenate(sums[3 * q : 3 * q + 3], axis=1).astype(BF16) for q in range(2)]

    stacked = jnp.concatenate(total(ya, y, ka, a3) + total(xb, x, kb, b3), axis=0)
    order = select_rows(
        64,
        64,
        lambda r: lax.div(lax.rem(r, 16), 8) * 32
        + lax.rem(lax.div(r, 2), 2) * 16
        + lax.rem(lax.div(r, 4), 2) * 8
        + lax.div(r, 16) * 2
        + lax.rem(r, 2),
    )
    zs[...] = dot(order, stacked, ((1,), (0,))).astype(BF16).reshape(4, 16, PIECE)
    z_last = []
    for d in (3, 2, 1):
        to = around(z, d)
        z_last.append((d, send(zs.at[to], zr.at[d - 1], device(z=to))))
    ring_poll(5)

    def down(s):
        lanes = slice(s * BLK, (s + 1) * BLK)
        pick = select_rows(64, BLK, lambda r: r + dp * 64)
        mine = dot(pick, act[:, :, lanes].reshape(512, BLK), ((1,), (1,))).astype(BF16)

        def one(k, carry):
            b = col_ref[k, 2 * mp + s]
            seen = jnp.concatenate([tokens(t, b) for t in (t0, t1, t2, t3)], axis=0)
            start = pl.multiple_of(k * BLK, BLK)
            dng_ref[s, :, pl.ds(start, BLK)] = dot(mine, seen, ((1,), (0,))).astype(BF16)
            return carry

        lax.fori_loop(0, KEPT, one, 0, unroll=8)

    down(0)
    down(1)
    ring_poll(6)

    for d, sem in z_last:
        arrive(sem, zr.at[d - 1])
    normed_grad = (
        zs[z].astype(F32) + zr[0].astype(F32) + zr[1].astype(F32) + zr[2].astype(F32)
    )
    scaled = normed_grad * gain16[...]
    unit_rows = unit16[...]
    pack[...] = inv16[:, 0:1] * (
        scaled - token_mean(scaled) - unit_rows * token_mean(scaled * unit_rows)
    )
    for p in range(PIECES):
        gin_ref[:, p * PIECE : (p + 1) * PIECE] = pack[2 * p : 2 * p + 2, :].astype(BF16)

    def z_order(r):
        at = lax.div(r, 32)
        near = lax.rem(lax.div(at, 4) + h, 2)
        return near * 128 + lax.div(lax.rem(r, 32), 2) * 8 + lax.rem(at, 4) * 2 + lax.rem(r, 2)

    order = select_rows(256, 256, z_order)
    for core in range(2):
        both = pg[2 * core : 2 * core + 2].reshape(256, 2 * BLK)
        pg_z[core] = dot(order, both, ((1,), (0,))).astype(BF16)

    def up_part(n, core, store):
        for s in range(SLOTS):
            grads = pg_z[core, :, s * BLK : (s + 1) * BLK]

            def one(k, carry):
                b = row_ref[dp * 4 + k, 2 * mp + s]
                picked = jnp.concatenate([n[:, 2 * b], n[:, 2 * b + 1]], axis=-1)
                store(s, k, dot(picked.reshape(BLK, BLK), grads, ((0,), (0,))))
                return carry

            lax.fori_loop(0, 4, one, 0, unroll=True)

    def keep(s, k, part):
        up_own[s, k] = part

    def finish_up(s, k, part):
        start = pl.multiple_of(k * BLK, BLK)
        upg_ref[s, pl.ds(start, BLK), :] = (up_own[s, k] + part).astype(BF16)

    up_part(n_own, 0, keep)
    for at, sem in nm_sib:
        arrive(sem, n_sib.at[at])
    up_part(n_sib, 1, finish_up)

    for copy in started:
        copy.wait_send()


def write_out(a, b, c, a_out, b_out, c_out, sem):
    copies = [
        pltpu.make_async_copy(src, dst, sem.at[k])
        for k, (src, dst) in enumerate([(a, a_out), (b, b_out), (c, c_out)])
    ]
    for copy in copies:
        copy.start()
    for copy in copies:
        copy.wait()


def local(
    inputs, out_grad, pre_act, norm_gain, up_weight, down_weight, row_blocks, col_blocks, counts
):
    vmem = pl.BlockSpec(memory_space=pltpu.VMEM)
    smem = pl.BlockSpec(memory_space=pltpu.SMEM)
    hbm = pl.BlockSpec(memory_space=pltpu.HBM)
    results = pl.pallas_call(
        kernel,
        out_shape=(
            pltpu.VMEM((2, FEATURES), BF16),
            pltpu.VMEM((SLOTS, 1024, BLK), BF16),
            pltpu.VMEM((SLOTS, 64, 4096), BF16),
        ),
        in_specs=[hbm, hbm, hbm, hbm, hbm, hbm, smem, smem, smem],
        out_specs=(vmem, vmem, vmem),
        scratch_shapes=[
            pltpu.VMEM((2, FEATURES), BF16),
            pltpu.VMEM((2, FEATURES), BF16),
            pltpu.VMEM((1, FEATURES), F32),
            pltpu.VMEM((SLOTS, KEPT + 1, BLK, BLK), BF16),
            pltpu.VMEM((SLOTS, BLK, 4096), BF16),
            pltpu.VMEM((128, 512), BF16),
            pltpu.VMEM((4, 128, 512), BF16),
            pltpu.VMEM((16, PIECE), F32),
            pltpu.VMEM((16, PIECE), F32),
            pltpu.VMEM((16, PIECE), F32),
            pltpu.VMEM((16, 128), F32),
            pltpu.VMEM((4, 16, PIECE), BF16),
            pltpu.VMEM((4, 16, PIECE), BF16),
            pltpu.VMEM((4, 4, 16, PIECE), BF16),
        ]
        + [pltpu.VMEM((LANES, 4, 4, 16, 128), BF16)] * 2
        + [pltpu.VMEM((2 * LANES, 128, 128), BF16)] * 4
        + [pltpu.VMEM((8, 2 * LANES, 32, 128), BF16)] * 2
        + [
            pltpu.VMEM((SLOTS, 384, BLK), F32),
            pltpu.VMEM((4, 128, 512), BF16),
            pltpu.VMEM((4, 128, 512), BF16),
            pltpu.VMEM((2, 256, 512), BF16),
            pltpu.VMEM((128, 512), BF16),
            pltpu.VMEM((SLOTS, 4, BLK, BLK), F32),
        ]
        + [pltpu.VMEM((4, 12, 32, BLK), BF16)] * 2
        + [pltpu.VMEM((3, 12, 32, BLK), BF16)] * 2
        + [pltpu.VMEM((4, 6, 16, BLK), BF16)] * 2
        + [pltpu.VMEM((3, 6, 16, BLK), BF16)] * 2
        + [
            pltpu.VMEM((4, 16, PIECE), BF16),
            pltpu.VMEM((3, 16, PIECE), BF16),
            pltpu.SMEM((48,), jnp.int32),
            pltpu.SemaphoreType.DMA((7,)),
            pltpu.SemaphoreType.DMA((N_COPIES,)),
            pltpu.SemaphoreType.DMA((N_COPIES,)),
        ],
        compiler_params=pltpu.CompilerParams(
            collective_id=0, has_side_effects=True, vmem_limit_bytes=56 * 1024 * 1024
        ),
    )(
        inputs,
        out_grad,
        pre_act,
        norm_gain.reshape(1, FEATURES),
        up_weight.reshape(SLOTS, KEPT, BLK, BLK),
        down_weight,
        row_blocks.T,
        col_blocks.T,
        counts,
    )
    return pl.pallas_call(
        write_out,
        out_shape=[jax.ShapeDtypeStruct(r.shape, r.dtype) for r in results],
        in_specs=[vmem] * 3,
        out_specs=[hbm] * 3,
        scratch_shapes=[pltpu.SemaphoreType.DMA((3,))],
        compiler_params=pltpu.CompilerParams(vmem_limit_bytes=8 * 1024 * 1024),
    )(*results)


def solution(mesh):
    placed = (
        P(("dp", "mp"), None),
        P(("dp", "mp"), None),
        P("dp", "mp"),
        P(),
        P("mp", None, None),
        P("mp", None, None),
        P(),
        P(),
        P(),
    )
    return jax.shard_map(
        local,
        mesh=mesh,
        in_specs=placed,
        out_specs=(P(("dp", "mp"), None), P("mp", "dp", None), P("mp", "dp", None)),
        check_vma=False,
    )
```

```python
import math

import jax
import jax.numpy as jnp
from jax import lax
from jax.experimental import pallas as pl
from jax.experimental.pallas import tpu as pltpu
from jax.sharding import PartitionSpec as P

EPS = 1e-06
F32 = jnp.float32
BF16 = jnp.bfloat16
PIECES = 8
PIECE = 768
BLK = 256
SLOTS = 2
KEPT = 16
FEATURES = 6144
LANES = 24
N_COPIES = 112


def dot(a, b, dims):
    return lax.dot_general(a, b, (dims, ((), ())), preferred_element_type=F32)


def select_rows(rows, columns, source_of):
    r = lax.broadcasted_iota(jnp.int32, (rows, columns), 0)
    c = lax.broadcasted_iota(jnp.int32, (rows, columns), 1)
    return (c == source_of(r)).astype(BF16)


def gelu_pair(z):
    a = math.sqrt(2.0 / math.pi)
    z2 = z * z
    t = jnp.tanh(a * z * (1.0 + 0.044715 * z2))
    half = 0.5 * (1.0 + t)
    slope = half + 0.5 * z * (1.0 - t * t) * (a * (1.0 + 3.0 * 0.044715 * z2))
    return z * half, slope


def kernel(
    x_hbm, og_hbm, pre_hbm, gain_hbm, up_hbm, dn_hbm, row_ref, col_ref, cnt_ref,
    gin_ref, upg_ref, dng_ref,
    x_ref, og_ref, gain_ref, up, dn, pre, pa,
    pack, gain16, unit16, inv16,
    raw_own, raw_oth, raw_nm,
    o_own, o_oth, t0, t1, t2, t3, n_own, n_sib,
    acc, act, pg, pg_z, pgb, up_own,
    ra, rb, ga, gb, ya, xb, ka, kb,
    zs, zr, pos,
    local_sem, send_sem, recv_sem,
):
    dp = lax.axis_index("dp")
    mp = lax.axis_index("mp")
    h, c = lax.div(dp, 2), lax.rem(dp, 2)
    z, x, y = lax.div(mp, 16), lax.rem(lax.div(mp, 4), 4), lax.rem(mp, 4)
    z8 = h * 4 + z

    def device(h=h, c=c, z=z, x=x, y=y):
        return {"dp": h * 2 + c, "mp": z * 16 + x * 4 + y}

    def around(at, by, n=4):
        return lax.rem(at + by + n, n)

    def z_device(at):
        return device(h=lax.div(at, 4), z=lax.rem(at, 4))

    x_peer = {d: device(x=around(x, d)) for d in (1, 2, 3)}
    y_peer = {d: device(y=around(y, d)) for d in (1, 2, 3)}
    z_plus, z_minus = z_device(around(z8, 1, 8)), z_device(around(z8, -1, 8))
    sibling = device(c=1 - c)
    partner = device(h=1 - h)

    started = []
    count = [0]

    def send(src, dst, target):
        k = count[0]
        count[0] += 1
        copy = pltpu.make_async_remote_copy(
            src_ref=src, dst_ref=dst, send_sem=send_sem.at[k], recv_sem=recv_sem.at[k],
            device_id=target, device_id_type=pl.DeviceIdType.MESH,
        )
        copy.start()
        started.append(copy)
        return k

    def arrive(k, dst):
        pltpu.make_async_remote_copy(
            src_ref=dst, dst_ref=dst, send_sem=send_sem.at[k], recv_sem=recv_sem.at[k],
            device_id=sibling, device_id_type=pl.DeviceIdType.MESH,
        ).wait_recv()

    def fetch(src, dst, k):
        copy = pltpu.make_async_copy(src, dst, local_sem.at[k])
        copy.start()
        return copy

    og_copy = fetch(og_hbm, og_ref, 0)
    x_copy = fetch(x_hbm, x_ref, 1)
    gain_copy = fetch(gain_hbm, gain_ref, 2)
    pre_copy = fetch(pre_hbm, pre, 3)

    barrier = pltpu.get_barrier_semaphore()
    greeted = [z_device(around(z8, k, 8)) for k in range(1, 8)]
    greeted += list(x_peer.values()) + list(y_peer.values()) + [sibling]
    for target in greeted:
        pl.semaphore_signal(
            barrier, inc=1, device_id=target, device_id_type=pl.DeviceIdType.MESH
        )

    weight_copies = [fetch(dn_hbm, dn, 4)]
    weight_copies += [fetch(up_hbm.at[s], up.at[s, pl.ds(0, KEPT)], 5 + s) for s in range(SLOTS)]

    og_copy.wait()
    for p in range(PIECES):
        pack[2 * p : 2 * p + 2, :] = og_ref[:, p * PIECE : (p + 1) * PIECE].astype(F32)
    raw_own[z] = pack[...].astype(BF16)
    x_copy.wait()
    gain_copy.wait()
    for p in range(PIECES):
        pack[2 * p : 2 * p + 2, :] = x_ref[:, p * PIECE : (p + 1) * PIECE].astype(F32)
        gain16[2 * p : 2 * p + 2, :] = jnp.broadcast_to(
            gain_ref[:, p * PIECE : (p + 1) * PIECE], (2, PIECE)
        )
    first = lax.rem(lax.broadcasted_iota(jnp.int32, (16, 1), 0), 2) == 0

    def token_mean(values):
        rows = jnp.sum(values, axis=1, keepdims=True)
        total0 = jnp.sum(jnp.where(first, rows, 0.0), axis=0, keepdims=True)
        total1 = jnp.sum(jnp.where(first, 0.0, rows), axis=0, keepdims=True)
        return jnp.where(first, total0, total1) * (1.0 / FEATURES)

    widened = pack[...]
    centred = widened - token_mean(widened)
    inv_std = lax.rsqrt(token_mean(centred * centred) + EPS)
    unit_rows = centred * inv_std
    unit16[...] = unit_rows
    inv16[...] = jnp.broadcast_to(inv_std, (16, 128))
    raw_nm[y, x] = (unit_rows * gain16[...]).astype(BF16)

    pl.semaphore_wait(barrier, len(greeted))

    own_z = [
        (d, send(raw_own.at[z], raw_own.at[z], device(z=around(z, d)))) for d in (1, 2, 3)
    ]
    cut_a, cut_b = pl.ds(0, PIECE // 2), pl.ds(PIECE // 2, PIECE // 2)
    a, b = raw_nm.at[y, x, :, cut_a], raw_nm.at[y, x, :, cut_b]
    nm_1 = [(d, send(a, a, x_peer[d]), send(b, b, y_peer[d])) for d in (1, 3, 2)]

    def place(raw, tiles, arrivals):
        for d, sem in arrivals:
            arrive(sem, raw.at[around(z, -d)])
        order = select_rows(
            64,
            64,
            lambda r: lax.div(lax.rem(r, 8), 2) * 16
            + lax.div(lax.rem(r, 16), 8) * 8
            + lax.div(r, 16) * 2
            + lax.rem(r, 2),
        )
        out = dot(order, raw[...].reshape(64, PIECE), ((1,), (0,))).astype(BF16)
        for p in range(4):
            for q in range(6):
                tiles[p * 6 + q, x, y] = out[16 * p : 16 * p + 16, 128 * q : 128 * q + 128]

    lane_a, lane_b = pl.ds(0, 12), pl.ds(12, 12)

    def narrow_send(o):
        a, b = o.at[lane_a, x, y], o.at[lane_b, x, y]
        return [(d, send(a, a, x_peer[d]), send(b, b, y_peer[d])) for d in (1, 3, 2)]

    def column_send(o, at_x, at_y):
        a, b = o.at[lane_a, at_x, y], o.at[lane_b, x, at_y]
        return [(d, send(a, a, y_peer[d]), send(b, b, x_peer[d])) for d in (1, 3, 2)]

    def narrow_wait(o, sem):
        d, sem_a, sem_b = sem
        arrive(sem_a, o.at[lane_a, around(x, -d), y])
        arrive(sem_b, o.at[lane_b, x, around(y, -d)])

    place(raw_own, o_own, own_z)
    own_n = narrow_send(o_own)
    own_w = [(0, column_send(o_own, x, y))]
    oth_z = [
        (d, send(raw_own.at[z], raw_oth.at[z], device(h=1 - h, z=around(z, d)))) for d in range(4)
    ]
    for d, sem_a, sem_b in nm_1:
        arrive(sem_a, raw_nm.at[y, around(x, -d), :, cut_a])
        arrive(sem_b, raw_nm.at[around(y, -d), x, :, cut_b])
    a, b = raw_nm.at[y, :, :, cut_a], raw_nm.at[:, x, :, cut_b]
    nm_2 = [(d, send(a, a, y_peer[d]), send(b, b, x_peer[d])) for d in (1, 3, 2)]

    pre_copy.wait()
    order = select_rows(
        128, 128, lambda r: lax.div(lax.rem(r, 8), 2) * 32 + lax.div(r, 8) * 2 + lax.rem(r, 2)
    )
    pa[0] = dot(order, pre[...], ((1,), (0,))).astype(BF16)
    pa_part = send(pa.at[0], pa.at[1], partner)
    pa_sib = send(pa.at[0], pa.at[2], sibling)

    for s in range(SLOTS):
        up[s, KEPT] = jnp.zeros((BLK, BLK), BF16)

    def locate(b, carry):
        for s in range(SLOTS):
            found = jnp.int32(KEPT)
            for k in range(KEPT):
                found = jnp.where(row_ref[k, 2 * mp + s] == b, k, found)
            pos[s * 24 + b] = found
        return carry

    lax.fori_loop(0, 24, locate, 0)
    for sem in own_n:
        narrow_wait(o_own, sem)
        own_w.append((sem[0], column_send(o_own, around(x, -sem[0]), around(y, -sem[0]))))

    for d, sem_a, sem_b in nm_2:
        arrive(sem_a, raw_nm.at[around(y, -d), :, :, cut_a])
        arrive(sem_b, raw_nm.at[:, around(x, -d), :, cut_b])
    order = select_rows(
        256,
        256,
        lambda r: lax.div(lax.rem(r, 8), 2) * 64
        + lax.div(lax.rem(r, 32), 8) * 16
        + lax.div(r, 32) * 2
        + lax.rem(r, 2),
    )
    out = dot(order, raw_nm[...].reshape(256, PIECE), ((1,), (0,))).astype(BF16)
    for p in range(PIECES):
        for q in range(6):
            n_own[z8, p * 6 + q] = out[32 * p : 32 * p + 32, 128 * q : 128 * q + 128]

    steps = [(0, 0), (0, 1), (1, 0), (1, 1), (2, 0), (2, 1), (3, 0)]
    halves = (pl.ds(0, 24), pl.ds(24, 24))
    nm_sems = {}

    def ring_send(n):
        far, half = steps[n]
        plus = n_own.at[around(z8, -far, 8), halves[half]]
        minus = n_own.at[around(z8, far, 8), halves[1 - half]]
        nm_sems[n] = (send(plus, plus, z_plus), send(minus, minus, z_minus))

    nm_sib = []

    def to_sibling(at):
        nm_sib.append((at, send(n_own.at[at], n_sib.at[at], sibling)))

    def ring_poll(n):
        far, half = steps[n]
        arrive(nm_sems[n][0], n_own.at[around(z8, -far - 1, 8), halves[half]])
        arrive(nm_sems[n][1], n_own.at[around(z8, far + 1, 8), halves[1 - half]])
        if n + 2 < len(steps):
            ring_send(n + 2)
        if half == 1:
            to_sibling(around(z8, far + 1, 8))
            to_sibling(around(z8, -far - 1, 8))
        if n == 6:
            to_sibling(around(z8, 4, 8))

    ring_send(0)
    ring_send(1)
    to_sibling(z8)

    place(raw_oth, o_oth, oth_z)
    oth_n = narrow_send(o_oth)
    for copy in weight_copies:
        copy.wait()
    for far, sems in own_w:
        for d, sem_a, sem_b in sems:
            arrive(sem_a, o_own.at[lane_a, around(x, -far), around(y, -d)])
            arrive(sem_b, o_own.at[lane_b, around(x, -d), around(y, -far)])
    for sem in oth_n:
        narrow_wait(o_oth, sem)

    def wide_send(o, lanes_a, lanes_b, from_x, from_y, d):
        a, b = o.at[lanes_a, :, from_y], o.at[lanes_b, from_x]
        return send(a, a, y_peer[d]), send(b, b, x_peer[d])

    def wide_wait(o, lanes_a, lanes_b, sems, d):
        arrive(sems[0], o.at[lanes_a, :, around(y, -d)])
        arrive(sems[1], o.at[lanes_b, around(x, -d)])

    oth_w = {d: wide_send(o_oth, lane_a, lane_b, x, y, d) for d in (1, 3, 2)}

    def oth_finish():
        for d in (1, 3, 2):
            wide_wait(o_oth, lane_a, lane_b, oth_w[d], d)

    ring_poll(0)

    def unpack(o, t):
        def one(k, carry):
            rows = o[k].astype(F32).reshape(16, 2, 8, 128)
            t[k] = rows[:, 0].reshape(128, 128).astype(BF16)
            t[LANES + k] = rows[:, 1].reshape(128, 128).astype(BF16)
            return carry

        lax.fori_loop(0, LANES, one, 0, unroll=4)

    unpack(o_own, t0)
    t_sib0 = send(t0, t2, sibling)

    live = [s < cnt_ref[mp] for s in range(SLOTS)]

    def tokens(t, b):
        return jnp.concatenate([t[2 * b], t[2 * b + 1]], axis=-1)

    def back(groups, between=lambda: None):
        rows = 128 * len(groups)
        for s in range(SLOTS):
            acc[s, 0:rows] = jnp.zeros((rows, BLK), F32)

            def grow(k, carry):
                parts = []
                for j in range(4):
                    b = col_ref[4 * k + j, 2 * mp + s]
                    parts.append(jnp.concatenate([tokens(t, b) for t in groups.values()], axis=0))
                start = pl.multiple_of(k * 1024, 1024)
                term = dot(
                    jnp.concatenate(parts, axis=1), dn[s, :, pl.ds(start, 1024)], ((1,), (1,))
                )

                acc[s, 0:rows] += term
                return carry

            lax.fori_loop(0, KEPT // 4, grow, 0, unroll=True)
            if s == 0:
                between()

        def derive(j, carry):
            at = pl.ds(pl.multiple_of(j * 16, 16), 16)
            for n, g in enumerate(groups):
                for s in range(SLOTS):
                    lanes = slice(s * BLK, (s + 1) * BLK)
                    value, slope = gelu_pair(pa[g, at, lanes].astype(F32))
                    grad = acc[s, pl.ds(pl.multiple_of(n * 128 + j * 16, 16), 16), :] * slope
                    pg[g, at, lanes] = jnp.where(live[s], grad, 0.0).astype(BF16)
                    act[g, at, lanes] = jnp.where(live[s], value, 0.0).astype(BF16)
            return carry

        lax.fori_loop(0, 8, derive, 0, unroll=4)

    back({0: t0}, lambda: ring_poll(1))

    order = select_rows(
        128, 128, lambda r: lax.div(lax.rem(r, 32), 8) * 32 + lax.div(r, 32) * 8 + lax.rem(r, 8)
    )
    pgb[...] = dot(order, pg[0], ((1,), (0,))).astype(BF16)

    def terms(source, out, base, first):
        def one(b, carry):
            weights = [up[s, pos[s * 24 + base + b]] for s in range(SLOTS)]
            term = dot(source, jnp.concatenate(weights, axis=1), ((1,), (1,))).astype(BF16)
            for q in range(4):
                out[q, b] = term[32 * q : 32 * q + 32]
            return carry

        lax.fori_loop(first, first + 6, one, 0, unroll=True)

    def reduce_send(r, at, g, peers, blocks):
        return [
            (d, send(r.at[around(at, d), blocks], g.at[d - 1, blocks], peers[d])) for d in (1, 3, 2)
        ]

    part0, part1 = pl.ds(0, 6), pl.ds(6, 6)
    terms(pg[0], ra, 0, 0)
    a1 = reduce_send(ra, x, ga, x_peer, part0)
    terms(pgb[...], rb, 12, 0)
    b1 = reduce_send(rb, y, gb, y_peer, part0)
    terms(pg[0], ra, 0, 6)
    a2 = reduce_send(ra, x, ga, x_peer, part1)
    terms(pgb[...], rb, 12, 6)
    b2 = reduce_send(rb, y, gb, y_peer, part1)
    ring_poll(2)
    arrive(pa_part, pa.at[1])
    pa_fwd = send(pa.at[1], pa.at[3], sibling)
    arrive(pa_sib, pa.at[2])
    arrive(t_sib0, t2)
    back({2: t2})
    ring_poll(3)
    oth_finish()
    unpack(o_oth, t1)
    t_sib1 = send(t1, t3, sibling)

    def collect(r, at, g, groups, blocks):
        for sems, part in groups:
            for d, sem in sems:
                arrive(sem, g.at[d - 1, part])
        return [
            r[at, j].astype(F32) + g[0, j].astype(F32) + g[1, j].astype(F32) + g[2, j].astype(F32)
            for j in range(blocks)
        ]

    def repack(sums, out):
        for j in range(6):
            for q in range(4):
                rows = slice(8 * q, 8 * q + 8)
                both = jnp.concatenate([sums[j][rows], sums[6 + j][rows]], axis=0)
                out[q, j] = both.astype(BF16)

    whole = pl.ds(0, 6)
    repack(collect(ra, x, ga, [(a1, part0), (a2, part1)], 12), ya)
    a3 = reduce_send(ya, y, ka, y_peer, whole)
    repack(collect(rb, y, gb, [(b1, part0), (b2, part1)], 12), xb)
    b3 = reduce_send(xb, x, kb, x_peer, whole)
    arrive(pa_fwd, pa.at[3])
    arrive(t_sib1, t3)
    back({1: t1, 3: t3}, lambda: ring_poll(4))

    def total(r, at, g, sems):
        sums = collect(r, at, g, [(sems, whole)], 6)
        return [jnp.concatenate(sums[3 * q : 3 * q + 3], axis=1).astype(BF16) for q in range(2)]

    stacked = jnp.concatenate(total(ya, y, ka, a3) + total(xb, x, kb, b3), axis=0)
    order = select_rows(
        64,
        64,
        lambda r: lax.div(lax.rem(r, 16), 8) * 32
        + lax.rem(lax.div(r, 2), 2) * 16
        + lax.rem(lax.div(r, 4), 2) * 8
        + lax.div(r, 16) * 2
        + lax.rem(r, 2),
    )
    zs[...] = dot(order, stacked, ((1,), (0,))).astype(BF16).reshape(4, 16, PIECE)
    z_last = []
    for d in (3, 2, 1):
        to = around(z, d)
        z_last.append((d, send(zs.at[to], zr.at[d - 1], device(z=to))))
    ring_poll(5)

    def down(s):
        lanes = slice(s * BLK, (s + 1) * BLK)
        pick = select_rows(64, BLK, lambda r: r + dp * 64)
        mine = dot(pick, act[:, :, lanes].reshape(512, BLK), ((1,), (1,))).astype(BF16)

        def one(k, carry):
            b = col_ref[k, 2 * mp + s]
            seen = jnp.concatenate([tokens(t, b) for t in (t0, t1, t2, t3)], axis=0)
            start = pl.multiple_of(k * BLK, BLK)
            dng_ref[s, :, pl.ds(start, BLK)] = dot(mine, seen, ((1,), (0,))).astype(BF16)
            return carry

        lax.fori_loop(0, KEPT, one, 0, unroll=8)

    down(0)
    down(1)
    ring_poll(6)

    for d, sem in z_last:
        arrive(sem, zr.at[d - 1])
    normed_grad = (
        zs[z].astype(F32) + zr[0].astype(F32) + zr[1].astype(F32) + zr[2].astype(F32)
    )
    scaled = normed_grad * gain16[...]
    unit_rows = unit16[...]
    pack[...] = inv16[:, 0:1] * (
        scaled - token_mean(scaled) - unit_rows * token_mean(scaled * unit_rows)
    )
    for p in range(PIECES):
        gin_ref[:, p * PIECE : (p + 1) * PIECE] = pack[2 * p : 2 * p + 2, :].astype(BF16)

    def z_order(r):
        at = lax.div(r, 32)
        near = lax.rem(lax.div(at, 4) + h, 2)
        return near * 128 + lax.div(lax.rem(r, 32), 2) * 8 + lax.rem(at, 4) * 2 + lax.rem(r, 2)

    order = select_rows(256, 256, z_order)
    for core in range(2):
        both = pg[2 * core : 2 * core + 2].reshape(256, 2 * BLK)
        pg_z[core] = dot(order, both, ((1,), (0,))).astype(BF16)

    def up_part(n, core, store):
        for s in range(SLOTS):
            grads = pg_z[core, :, s * BLK : (s + 1) * BLK]

            def one(k, carry):
                b = row_ref[dp * 4 + k, 2 * mp + s]
                picked = jnp.concatenate([n[:, 2 * b], n[:, 2 * b + 1]], axis=-1)
                store(s, k, dot(picked.reshape(BLK, BLK), grads, ((0,), (0,))))
                return carry

            lax.fori_loop(0, 4, one, 0, unroll=True)

    def keep(s, k, part):
        up_own[s, k] = part

    def finish_up(s, k, part):
        start = pl.multiple_of(k * BLK, BLK)
        upg_ref[s, pl.ds(start, BLK), :] = (up_own[s, k] + part).astype(BF16)

    up_part(n_own, 0, keep)
    for at, sem in nm_sib:
        arrive(sem, n_sib.at[at])
    up_part(n_sib, 1, finish_up)

    for copy in started:
        copy.wait_send()


def write_out(a, b, c, a_out, b_out, c_out, sem):
    copies = [
        pltpu.make_async_copy(src, dst, sem.at[k])
        for k, (src, dst) in enumerate([(a, a_out), (b, b_out), (c, c_out)])
    ]
    for copy in copies:
        copy.start()
    for copy in copies:
        copy.wait()


def local(
    inputs, out_grad, pre_act, norm_gain, up_weight, down_weight, row_blocks, col_blocks, counts
):
    vmem = pl.BlockSpec(memory_space=pltpu.VMEM)
    smem = pl.BlockSpec(memory_space=pltpu.SMEM)
    hbm = pl.BlockSpec(memory_space=pltpu.HBM)
    results = pl.pallas_call(
        kernel,
        out_shape=(
            pltpu.VMEM((2, FEATURES), BF16),
            pltpu.VMEM((SLOTS, 1024, BLK), BF16),
            pltpu.VMEM((SLOTS, 64, 4096), BF16),
        ),
        in_specs=[hbm, hbm, hbm, hbm, hbm, hbm, smem, smem, smem],
        out_specs=(vmem, vmem, vmem),
        scratch_shapes=[
            pltpu.VMEM((2, FEATURES), BF16),
            pltpu.VMEM((2, FEATURES), BF16),
            pltpu.VMEM((1, FEATURES), F32),
            pltpu.VMEM((SLOTS, KEPT + 1, BLK, BLK), BF16),
            pltpu.VMEM((SLOTS, BLK, 4096), BF16),
            pltpu.VMEM((128, 512), BF16),
            pltpu.VMEM((4, 128, 512), BF16),
            pltpu.VMEM((16, PIECE), F32),
            pltpu.VMEM((16, PIECE), F32),
            pltpu.VMEM((16, PIECE), F32),
            pltpu.VMEM((16, 128), F32),
            pltpu.VMEM((4, 16, PIECE), BF16),
            pltpu.VMEM((4, 16, PIECE), BF16),
            pltpu.VMEM((4, 4, 16, PIECE), BF16),
        ]
        + [pltpu.VMEM((LANES, 4, 4, 16, 128), BF16)] * 2
        + [pltpu.VMEM((2 * LANES, 128, 128), BF16)] * 4
        + [pltpu.VMEM((8, 2 * LANES, 32, 128), BF16)] * 2
        + [
            pltpu.VMEM((SLOTS, 384, BLK), F32),
            pltpu.VMEM((4, 128, 512), BF16),
            pltpu.VMEM((4, 128, 512), BF16),
            pltpu.VMEM((2, 256, 512), BF16),
            pltpu.VMEM((128, 512), BF16),
            pltpu.VMEM((SLOTS, 4, BLK, BLK), F32),
        ]
        + [pltpu.VMEM((4, 12, 32, BLK), BF16)] * 2
        + [pltpu.VMEM((3, 12, 32, BLK), BF16)] * 2
        + [pltpu.VMEM((4, 6, 16, BLK), BF16)] * 2
        + [pltpu.VMEM((3, 6, 16, BLK), BF16)] * 2
        + [
            pltpu.VMEM((4, 16, PIECE), BF16),
            pltpu.VMEM((3, 16, PIECE), BF16),
            pltpu.SMEM((48,), jnp.int32),
            pltpu.SemaphoreType.DMA((7,)),
            pltpu.SemaphoreType.DMA((N_COPIES,)),
            pltpu.SemaphoreType.DMA((N_COPIES,)),
        ],
        compiler_params=pltpu.CompilerParams(
            collective_id=0, has_side_effects=True, vmem_limit_bytes=56 * 1024 * 1024
        ),
    )(
        inputs,
        out_grad,
        pre_act,
        norm_gain.reshape(1, FEATURES),
        up_weight.reshape(SLOTS, KEPT, BLK, BLK),
        down_weight,
        row_blocks.T,
        col_blocks.T,
        counts,
    )
    return pl.pallas_call(
        write_out,
        out_shape=[jax.ShapeDtypeStruct(r.shape, r.dtype) for r in results],
        in_specs=[vmem] * 3,
        out_specs=[hbm] * 3,
        scratch_shapes=[pltpu.SemaphoreType.DMA((3,))],
        compiler_params=pltpu.CompilerParams(vmem_limit_bytes=8 * 1024 * 1024),
    )(*results)


def solution(mesh):
    placed = (
        P(("dp", "mp"), None),
        P(("dp", "mp"), None),
        P("dp", "mp"),
        P(),
        P("mp", None, None),
        P("mp", None, None),
        P(),
        P(),
        P(),
    )
    return jax.shard_map(
        local,
        mesh=mesh,
        in_specs=placed,
        out_specs=(P(("dp", "mp"), None), P("mp", "dp", None), P("mp", "dp", None)),
        check_vma=False,
    )
```
